512 devices in a mesh: wide: 64 (over y_hi, z, core), tp: 8 (over x, y_lo).
Axes of the slice: x: 4, y: 8 (y_hi: 4, y_lo: 2; y = y_hi * 2 + y_lo), z: 8, core: 2. Of those that a mesh axis runs over, the one named last changes fastest.
Arguments:
- queries: bfloat16 [64, 128, 128], P('wide', 'tp'), may hold values from -384 to 384, as said below
- new_keys: bfloat16 [64, 8, 128], P('wide', 'tp'), may hold values from -9 to 9
- new_values: bfloat16 [64, 8, 128], P('wide', 'tp'), may hold values from -6 to 6
- prefix_keys: bfloat16 [256, 128, 8, 128], P('wide', None, 'tp'), may hold values from -6 to 6
- prefix_values: bfloat16 [256, 128, 8, 128], P('wide', None, 'tp'), may hold values from -6 to 6
- suffix_keys: bfloat16 [64, 512, 8, 128], P('wide', None, 'tp'), may hold values from -6 to 6
- suffix_values: bfloat16 [64, 512, 8, 128], P('wide', None, 'tp'), may hold values from -6 to 6
- lengths: int32 [64], P('wide'), may hold values from 1 to 512, as said below
- page_table: int32 [128], replicated, may hold values from 0 to 255, as said below
- out_weight: bfloat16 [16384, 16384], P('tp', 'wide'), may hold values from -3.59375 to 3.59375
Outputs:
- mixed: float32 [64, 16384], P('tp', 'wide')
The draws below stay inside these ranges and needn't reach their ends.
Inputs may be any that keep to these rules, and one draw needn't show every extreme that they name: `queries`: at most 384 in magnitude. `lengths`: some request has exactly 512 live slots. `page_table`: distinct pages; page 0 and page 256 - 1 are always among them.
All inputs are finite; a program needn't handle non-finite values.
Results may differ from the reference program's by a relative error of at most 0.013.
Values may be sent and summed in bfloat16 or wider, within the bound.
A program may use at most 128 MiB of HBM per device.

```python
import jax
import jax.numpy as jnp
from jax import lax

D = 16384
QH = 128
KVH = 8
HD = 128
GROUP = 16
REQUESTS = 64
SUF = 512
BLK = 128
NBLK = 128
PAGES = 256


def shared_queries(key):
    base_key = jax.random.fold_in(key, 7)
    return jax.random.truncated_normal(base_key, -6.0, 6.0, (REQUESTS, QH, HD), jnp.float32)


def draw_queries(key, part):
    values = shared_queries(key)
    return values.astype(jnp.bfloat16)


def draw_new_keys(key, part):
    key = jax.random.fold_in(key, 14)
    noise_key = jax.random.fold_in(key, 1)
    noise = jax.random.truncated_normal(noise_key, -6.0, 6.0, (REQUESTS, KVH, HD), jnp.float32)
    values = noise
    return values.astype(jnp.bfloat16)


def draw_lengths(key, part):
    key = jax.random.fold_in(key, 12)
    first_key = jax.random.fold_in(key, 1)
    second_key = jax.random.fold_in(key, 2)
    drawn = jax.random.randint(first_key, (REQUESTS,), 1, SUF + 1)
    chosen = jax.random.randint(second_key, (), 0, REQUESTS)
    return jnp.where(jnp.arange(REQUESTS) == chosen, SUF, drawn).astype(jnp.int32)


def draw_page_table(key, part):
    key = jax.random.fold_in(key, 13)
    first_key = jax.random.fold_in(key, 1)
    second_key = jax.random.fold_in(key, 2)
    inner = 1 + jax.random.permutation(first_key, PAGES - 2)[:NBLK - 2]
    table = jnp.concatenate([jnp.zeros((1,), jnp.int32), inner.astype(jnp.int32), jnp.full((1,), PAGES - 1, jnp.int32)])
    order = jax.random.permutation(second_key, NBLK)
    return table[order].astype(jnp.int32)


def shard_levels(rng, extent, shards, least, high):
    def one(axis_at, blocks):
        heights = jax.random.uniform(jax.random.fold_in(jax.random.fold_in(rng, 6), axis_at), (blocks,), jnp.float32, least / len(shards), high / len(shards))
        return jnp.repeat(jnp.exp(heights), extent[axis_at] // blocks).reshape((-1,) + (1,) * (len(extent) - axis_at - 1))

    loudness = one(*shards[0])
    for cut in shards[1:]:
        loudness = loudness * one(*cut)
    return loudness


def scatter_about(stream_key, extent, width, bound, shards=(), held_as=jnp.bfloat16):
    entries = width * jax.random.normal(stream_key, extent, jnp.float32)
    if shards:
        entries = entries * shard_levels(stream_key, extent, shards, -0.22, 0.18)
    return jnp.clip(entries, -bound, bound).astype(held_as)


def setup_inputs(seed: int = 0) -> dict:
    streams_of = jax.random.split(jax.random.key(seed), 11)
    return {
        "queries": draw_queries(jax.random.fold_in(streams_of[10], 71), 0),
        "new_keys": draw_new_keys(jax.random.fold_in(streams_of[10], 71), 0),
        "new_values": scatter_about(streams_of[2], (REQUESTS, KVH, HD), 1.0, 6.0, ((0, 64), (1, 8))),
        "prefix_keys": scatter_about(streams_of[3], (PAGES, BLK, KVH, HD), 1.0, 6.0, ((0, 64), (2, 8))),
        "prefix_values": scatter_about(streams_of[4], (PAGES, BLK, KVH, HD), 1.0, 6.0, ((0, 64), (2, 8))),
        "suffix_keys": scatter_about(streams_of[5], (REQUESTS, SUF, KVH, HD), 1.0, 6.0, ((0, 64), (2, 8))),
        "suffix_values": scatter_about(streams_of[6], (REQUESTS, SUF, KVH, HD), 1.0, 6.0, ((0, 64), (2, 8))),
        "lengths": draw_lengths(jax.random.fold_in(streams_of[10], 71), 0),
        "page_table": draw_page_table(jax.random.fold_in(streams_of[10], 71), 0),
        "out_weight": scatter_about(streams_of[9], (QH * HD, D), 0.6, 3.59375, ((0, 8), (1, 64))),
    }


def reference(queries, new_keys, new_values, prefix_keys, prefix_values, suffix_keys, suffix_values, lengths, page_table, out_weight):
    score_scale = HD ** -0.5
    used_keys = prefix_keys[page_table].reshape(NBLK * BLK, KVH, HD).astype(jnp.float32)
    used_values = prefix_values[page_table].reshape(NBLK * BLK, KVH, HD).astype(jnp.float32)
    positions = jnp.arange(SUF, dtype=jnp.int32)

    def per_request(items):
        query, new_key, new_value, suf_keys, suf_values, length = items
        query = query.astype(jnp.float32).reshape(KVH, GROUP, HD)
        pre_scores = jnp.einsum('ghd,ngd->ghn', query, used_keys) * score_scale
        live = positions < length
        suf_scores = jnp.einsum('ghd,sgd->ghs', query, suf_keys.astype(jnp.float32)) * score_scale
        suf_scores = jnp.where(live[None, None, :], suf_scores, -1e30)
        own_score = jnp.einsum('ghd,gd->gh', query, new_key.astype(jnp.float32)) * score_scale
        row_max = jnp.maximum(jnp.maximum(jnp.max(pre_scores, axis=-1), jnp.max(suf_scores, axis=-1)), own_score)
        pre_weights = jnp.exp(pre_scores - row_max[..., None])
        suf_weights = jnp.where(live[None, None, :], jnp.exp(suf_scores - row_max[..., None]), 0.0)
        own_weight = jnp.exp(own_score - row_max)
        total = jnp.sum(pre_weights, axis=-1) + jnp.sum(suf_weights, axis=-1) + own_weight
        pre_round = lax.optimization_barrier(pre_weights.astype(jnp.bfloat16)).astype(jnp.float32)
        suf_round = lax.optimization_barrier(suf_weights.astype(jnp.bfloat16)).astype(jnp.float32)
        own_round = lax.optimization_barrier(own_weight.astype(jnp.bfloat16)).astype(jnp.float32)
        summed = jnp.einsum('ghn,ngd->ghd', pre_round, used_values)
        summed = summed + jnp.einsum('ghs,sgd->ghd', suf_round, suf_values.astype(jnp.float32))
        summed = summed + own_round[..., None] * new_value.astype(jnp.float32)[:, None, :]
        return (summed / total[..., None]).astype(jnp.bfloat16).reshape(QH * HD)

    attn = lax.map(per_request, (queries, new_keys, new_values, suffix_keys, suffix_values, lengths))
    return jnp.dot(attn, out_weight, preferred_element_type=jnp.float32)
```

```python
import functools

import jax
import jax.numpy as jnp
from jax import lax
from jax.experimental import pallas as pl
from jax.experimental.pallas import tpu as pltpu
from jax.sharding import PartitionSpec as P

MESH = pl.DeviceIdType.MESH
NY, NZ = 4, 8
NX, NL = 4, 2
CHIPS = NY * NZ
WIDE = [(a, b) for a in (2, 1, 3, 0) for b in (4, 3, 5, 2, 6, 1, 7, 0) if (a, b) != (0, 0)]
TP = [(a, b, d) for a in (2, 1, 3, 0) for b in (1, 0) for d in (1, 0) if (a, b, d) != (0, 0, 0)]
LOG2E = 1.4426950408889634


def kernel(
    len_ref,
    q_hbm,
    nk_hbm,
    nv_hbm,
    pk_hbm,
    pv_hbm,
    sk_hbm,
    sv_hbm,
    pt_hbm,
    w_hbm,
    o_ref,
    qbuf,
    kbuf,
    vbuf,
    ktbuf,
    skbuf,
    svbuf,
    nkbuf,
    nvbuf,
    ptbuf,
    wbuf,
    acc_out,
    st_out,
    acc_in,
    st_in,
    attn_buf,
    attn32,
    proj_out,
    proj_in,
    local_sem,
    q_send,
    q_recv,
    core_send,
    core_recv,
    acc_send,
    acc_recv,
    st_send,
    st_recv,
    attn_send,
    attn_recv,
    proj_send,
    proj_recv,
):
    heads, hd = q_hbm.shape
    tokens = pk_hbm.shape[0]
    rows = NZ * heads
    scale = hd ** (-0.5) * LOG2E
    wide = lax.axis_index("wide")
    tp = lax.axis_index("tp")
    y, z, c = wide // (2 * NZ), (wide // 2) % NZ, wide % 2
    x, low = tp // NL, tp % NL

    def wide_at(a, b, sign=1):
        return (((y + sign * a + NY) % NY) * (2 * NZ) + ((z + sign * b + NZ) % NZ) * 2 + c, tp)

    def tp_at(a, b, d):
        return (wide - c + (c + d) % 2, ((x + a) % NX) * NL + (low + b) % NL)

    partner = tp_at(0, 0, 1)

    barrier = pltpu.get_barrier_semaphore()
    for a, b in WIDE:
        pl.semaphore_signal(barrier, inc=1, device_id=wide_at(a, b), device_id_type=MESH)
    for a, b, d in TP:
        pl.semaphore_signal(barrier, inc=1, device_id=tp_at(a, b, d), device_id_type=MESH)

    loads = [
        (q_hbm, qbuf.at[0, pl.ds(0, heads)]),
        (sk_hbm, skbuf),
        (sv_hbm, svbuf),
        (nk_hbm, nkbuf),
        (nv_hbm, nvbuf),
        (pt_hbm, ptbuf),
        (pk_hbm, kbuf.at[0]),
        (pv_hbm, vbuf.at[0]),
        (w_hbm, wbuf.at[0]),
    ]
    loads = [pltpu.make_async_copy(src, dst, local_sem.at[i]) for i, (src, dst) in enumerate(loads)]
    for load in loads:
        load.start()
    for load in loads[:6]:
        load.wait()

    own_q = qbuf[0, :heads]
    length = len_ref[0]
    slots = skbuf.shape[0]
    scores = lax.dot_general(
        own_q, skbuf[...], (((1,), (1,)), ((), ())), preferred_element_type=jnp.float32
    )
    live = lax.broadcasted_iota(jnp.int32, (heads, slots), 1) < length
    scores = jnp.where(live, scores, -1e30)
    new_score = jnp.sum(
        own_q.astype(jnp.float32) * nkbuf[...].astype(jnp.float32), axis=1, keepdims=True
    )
    suf_max = jnp.maximum(jnp.max(scores, axis=1, keepdims=True), new_score)
    weights = jnp.exp2((scores - suf_max) * scale)
    new_weight = jnp.exp2((new_score - suf_max) * scale)
    suf_mass = jnp.sum(weights, axis=1, keepdims=True) + new_weight
    suf_acc = jnp.dot(weights.astype(jnp.bfloat16), svbuf[...], preferred_element_type=jnp.float32)
    suf_acc = suf_acc + new_weight.astype(jnp.bfloat16).astype(jnp.float32) * nvbuf[...].astype(
        jnp.float32
    )
    suf_max = suf_max * scale

    pages = tokens // 128
    bias = []
    for half in range(2):
        first = (wide - c + (c + half) % 2) * pages
        for page in range(pages):
            used = jnp.max((ptbuf[...] == first + page).astype(jnp.float32), axis=1, keepdims=True)
            bias.append(jnp.broadcast_to((used - 1.0) * 1e30, (1, 128)))
    bias = jnp.concatenate(bias, axis=1)

    for load in loads[6:]:
        load.wait()
    ktbuf[:, :tokens] = kbuf[0].T

    pl.semaphore_wait(barrier, len(WIDE) + len(TP))

    for a, b in WIDE:
        pltpu.make_async_remote_copy(
            qbuf.at[0, pl.ds(0, heads)],
            qbuf.at[a, pl.ds(b * heads, heads)],
            q_send,
            q_recv.at[a],
            device_id=wide_at(a, b),
            device_id_type=MESH,
        ).start()
    swaps = [
        pltpu.make_async_remote_copy(
            buf.at[0],
            buf.at[1],
            core_send.at[i],
            core_recv.at[i],
            device_id=partner,
            device_id_type=MESH,
        )
        for i, buf in enumerate((kbuf, vbuf, wbuf))
    ]
    for swap in swaps:
        swap.start()
    swaps[0].wait_recv()
    ktbuf[:, tokens:] = kbuf[1].T
    swaps[1].wait_recv()
    values = vbuf[...].reshape(2 * tokens, hd)

    def landed(ref, sem):
        pltpu.make_async_copy(ref, ref, sem).wait()

    lane = lax.broadcasted_iota(jnp.int32, (rows, 128), 1)
    for a in (0, 1, 3, 2):
        landed(qbuf.at[0, pl.ds(heads, rows - heads)] if a == 0 else qbuf.at[a], q_recv.at[a])
        s = jnp.dot(qbuf[a], ktbuf[...], preferred_element_type=jnp.float32) + bias
        top = jnp.max(s, axis=1, keepdims=True)
        p = jnp.exp2((s - top) * scale)
        mass = jnp.sum(p, axis=1, keepdims=True)
        acc = jnp.dot(p.astype(jnp.bfloat16), values, preferred_element_type=jnp.float32)
        acc_out[a] = acc.astype(jnp.bfloat16)
        stats = jnp.where(lane == 0, top * scale, jnp.where(lane == 1, mass, 0.0))
        st_out[a] = stats.T[:2]
        for b in (4, 3, 5, 2, 6, 1, 7, 0):
            if (a, b) == (0, 0):
                continue
            pltpu.make_async_remote_copy(
                st_out.at[a],
                st_in.at[a, b],
                st_send,
                st_recv.at[a],
                device_id=wide_at(a, b, -1),
                device_id_type=MESH,
            ).start()
            pltpu.make_async_remote_copy(
                acc_out.at[a, pl.ds(b * heads, heads)],
                acc_in.at[a, pl.ds(b * heads, heads)],
                acc_send,
                acc_recv.at[a],
                device_id=wide_at(a, b, -1),
                device_id_type=MESH,
            ).start()
        if a == 0:
            acc_in[0, :heads] = acc_out[0, :heads]
            st_in[0, 0] = st_out[0]

    spot = lax.broadcasted_iota(jnp.int32, (2, rows), 1) // heads
    joined = []
    for a in range(NY):
        landed(st_in.at[0, pl.ds(1, NZ - 1)] if a == 0 else st_in.at[a], st_recv.at[a])
        line = jnp.zeros((2, rows), jnp.float32)
        for b in range(NZ):
            line = jnp.where(spot == b, st_in[a, b], line)
        joined.append(line)
    tops = jnp.concatenate([line[:1] for line in joined], axis=0)
    masses = jnp.concatenate([line[1:] for line in joined], axis=0)
    best = jnp.broadcast_to(jnp.max(tops, axis=0, keepdims=True), (8, rows))
    for shift in (heads, 2 * heads, 4 * heads):
        best = jnp.maximum(best, pltpu.roll(best, shift, 1))
    factors = jnp.exp2(tops - best[:1])
    mass_line = jnp.sum(factors * masses, axis=0, keepdims=True)
    mine = lax.broadcasted_iota(jnp.int32, (heads, rows), 1) % heads == lax.broadcasted_iota(
        jnp.int32, (heads, rows), 0
    )
    pre_max = jnp.max(jnp.where(mine, best[:1], -3e38), axis=1, keepdims=True)
    pre_mass = jnp.sum(jnp.where(mine, mass_line, 0.0), axis=1, keepdims=True)
    pre_acc = jnp.zeros((2 * heads, hd), jnp.float32)
    for a in range(NY):
        spread = jnp.where(mine, factors[a : a + 1], 0.0)
        high = spread.astype(jnp.bfloat16)
        rest = (spread - high.astype(jnp.float32)).astype(jnp.bfloat16)
        landed(acc_in.at[0, pl.ds(heads, rows - heads)] if a == 0 else acc_in.at[a], acc_recv.at[a])
        pre_acc = pre_acc + jnp.dot(
            jnp.concatenate([high, rest], axis=0), acc_in[a], preferred_element_type=jnp.float32
        )
    row_max = jnp.maximum(pre_max, suf_max)
    pre_factor = jnp.exp2(pre_max - row_max)
    suf_factor = jnp.exp2(suf_max - row_max)
    total = pre_mass * pre_factor + suf_mass * suf_factor
    summed = (pre_acc[:heads] + pre_acc[heads:]) * pre_factor + suf_acc * suf_factor
    own_rows = pl.ds(pl.multiple_of((y * NZ + z) * heads, heads), heads)
    attn_buf[own_rows, :] = (summed / total).astype(jnp.bfloat16)

    for a, b in WIDE:
        pltpu.make_async_remote_copy(
            attn_buf.at[own_rows],
            attn_buf.at[own_rows],
            attn_send,
            attn_recv,
            device_id=wide_at(a, b),
            device_id_type=MESH,
        ).start()
    swaps[2].wait_recv()
    landed(attn_buf.at[pl.ds(0, (CHIPS - 1) * heads)], attn_recv)

    attn32[...] = attn_buf[...].astype(jnp.float32)
    columns = w_hbm.shape[1]
    sums = [jnp.zeros((CHIPS, columns), jnp.float32) for _ in range(2)]
    for h in range(0, heads, 2):
        pair = jnp.concatenate(
            [attn32[pl.ds(h + i, CHIPS, stride=heads), :] for i in range(2)], axis=1
        ).astype(jnp.bfloat16)
        for d in range(2):
            sums[d] = sums[d] + jnp.dot(
                pair, wbuf[d, h * hd : (h + 2) * hd, :], preferred_element_type=jnp.float32
            )
    share = CHIPS // (NX * NL)
    for d in range(2):
        for t in range(NX * NL):
            part = sums[d][t * share : (t + 1) * share]
            proj_out[d, t] = jnp.concatenate([part[:, :128], part[:, 128:]], axis=0)
    for i, (a, b, d) in enumerate(TP):
        target = tp_at(a, b, d)
        pltpu.make_async_remote_copy(
            proj_out.at[d, target[1]],
            proj_in.at[i],
            proj_send,
            proj_recv,
            device_id=target,
            device_id_type=MESH,
        ).start()
    landed(proj_in, proj_recv)
    parts = [proj_out[0, tp], jnp.zeros((8, 128), jnp.float32)]
    for i, (a, b, d) in enumerate(TP):
        parts[d] = parts[d] + proj_in[i]
    for core in range(2):
        half = jnp.where(c == core, parts[0], parts[1])
        for i in range(share):
            for j in range(2):
                o_ref[2 * i + core : 2 * i + core + 1, j * 128 : (j + 1) * 128] = half[
                    j * share + i : j * share + i + 1
                ]

    landed(qbuf.at[pl.ds(0, NY - 1)], q_send)
    landed(qbuf.at[0, pl.ds(heads, rows - heads)], q_send)
    for swap in swaps:
        swap.wait_send()
    landed(acc_out.at[pl.ds(0, NY - 1)], acc_send)
    landed(acc_out.at[0, pl.ds(heads, rows - heads)], acc_send)
    landed(st_in.at[pl.ds(0, NY - 1)], st_send)
    landed(st_in.at[0, pl.ds(1, NZ - 1)], st_send)
    landed(attn_buf.at[pl.ds(0, (CHIPS - 1) * heads)], attn_send)
    landed(proj_in, proj_send)


def local(
    queries,
    new_keys,
    new_values,
    prefix_keys,
    prefix_values,
    suffix_keys,
    suffix_values,
    lengths,
    page_table,
    out_weight,
):
    _, heads, hd = queries.shape
    tokens = prefix_keys.shape[0] * prefix_keys.shape[1]
    slots = suffix_keys.shape[1]
    depth, columns = out_weight.shape
    rows = NZ * heads
    bf16, f32 = jnp.bfloat16, jnp.float32
    dma = pltpu.SemaphoreType.DMA
    return pl.pallas_call(
        kernel,
        out_shape=jax.ShapeDtypeStruct((8, columns), f32),
        in_specs=[pl.BlockSpec(memory_space=pltpu.SMEM)] + [pl.BlockSpec(memory_space=pl.ANY)] * 9,
        out_specs=pl.BlockSpec(memory_space=pltpu.VMEM),
        scratch_shapes=[
            pltpu.VMEM((NY, rows, hd), bf16),
            pltpu.VMEM((2, tokens, hd), bf16),
            pltpu.VMEM((2, tokens, hd), bf16),
            pltpu.VMEM((hd, 2 * tokens), bf16),
            pltpu.VMEM((slots, hd), bf16),
            pltpu.VMEM((slots, hd), bf16),
            pltpu.VMEM((1, hd), bf16),
            pltpu.VMEM((1, hd), bf16),
            pltpu.VMEM((1, page_table.shape[0]), jnp.int32),
            pltpu.VMEM((2, depth, columns), bf16),
            pltpu.VMEM((NY, rows, hd), bf16),
            pltpu.VMEM((NY, 2, rows), f32),
            pltpu.VMEM((NY, rows, hd), bf16),
            pltpu.VMEM((NY, NZ, 2, rows), f32),
            pltpu.VMEM((CHIPS * heads, hd), bf16),
            pltpu.VMEM((CHIPS * heads, hd), f32),
            pltpu.VMEM((2, NX * NL, 8, 128), f32),
            pltpu.VMEM((len(TP), 8, 128), f32),
            dma((9,)),
            dma,
            dma((NY,)),
            dma((3,)),
            dma((3,)),
            dma,
            dma((NY,)),
            dma,
            dma((NY,)),
            dma,
            dma,
            dma,
            dma,
        ],
        compiler_params=pltpu.CompilerParams(
            collective_id=0, has_side_effects=True, vmem_limit_bytes=32 * 1024 * 1024
        ),
        name="attention_step",
    )(
        lengths,
        queries.reshape(heads, hd),
        new_keys.reshape(1, hd),
        new_values.reshape(1, hd),
        prefix_keys.reshape(tokens, hd),
        prefix_values.reshape(tokens, hd),
        suffix_keys.reshape(slots, hd),
        suffix_values.reshape(slots, hd),
        page_table.reshape(1, -1),
        out_weight,
    )


def solution(mesh):
    in_specs = (
        P("wide", "tp", None),
        P("wide", "tp", None),
        P("wide", "tp", None),
        P("wide", None, "tp", None),
        P("wide", None, "tp", None),
        P("wide", None, "tp", None),
        P("wide", None, "tp", None),
        P("wide"),
        P(),
        P("tp", "wide"),
    )
    out_specs = P("tp", "wide")
    return jax.shard_map(local, mesh=mesh, in_specs=in_specs, out_specs=out_specs, check_vma=False)
```

```python
import functools

import jax
import jax.numpy as jnp
from jax import lax
from jax.experimental import pallas as pl
from jax.experimental.pallas import tpu as pltpu
from jax.sharding import PartitionSpec as P

MESH = pl.DeviceIdType.MESH
NY, NZ = 4, 8
NX, NL = 4, 2
CHIPS = NY * NZ
WIDE = [(a, b) for a in (2, 1, 3, 0) for b in (4, 3, 5, 2, 6, 1, 7, 0) if (a, b) != (0, 0)]
TP = [(a, b, d) for a in (2, 1, 3, 0) for b in (1, 0) for d in (1, 0) if (a, b, d) != (0, 0, 0)]
LOG2E = 1.4426950408889634


def kernel(
    len_ref,
    q_hbm,
    nk_hbm,
    nv_hbm,
    pk_hbm,
    pv_hbm,
    sk_hbm,
    sv_hbm,
    pt_hbm,
    w_hbm,
    o_ref,
    qbuf,
    kbuf,
    vbuf,
    ktbuf,
    skbuf,
    svbuf,
    nkbuf,
    nvbuf,
    ptbuf,
    wbuf,
    acc_out,
    st_out,
    acc_in,
    st_in,
    attn_buf,
    attn32,
    proj_out,
    proj_in,
    local_sem,
    q_send,
    q_recv,
    core_send,
    core_recv,
    acc_send,
    acc_recv,
    st_send,
    st_recv,
    attn_send,
    attn_recv,
    proj_send,
    proj_recv,
):
    heads, hd = q_hbm.shape
    tokens = pk_hbm.shape[0]
    rows = NZ * heads
    scale = hd ** (-0.5) * LOG2E
    wide = lax.axis_index("wide")
    tp = lax.axis_index("tp")
    y, z, c = wide // (2 * NZ), (wide // 2) % NZ, wide % 2
    x, low = tp // NL, tp % NL

    def wide_at(a, b, sign=1):
        return (((y + sign * a + NY) % NY) * (2 * NZ) + ((z + sign * b + NZ) % NZ) * 2 + c, tp)

    def tp_at(a, b, d):
        return (wide - c + (c + d) % 2, ((x + a) % NX) * NL + (low + b) % NL)

    partner = tp_at(0, 0, 1)

    barrier = pltpu.get_barrier_semaphore()
    for a, b in WIDE:
        pl.semaphore_signal(barrier, inc=1, device_id=wide_at(a, b), device_id_type=MESH)
    for a, b, d in TP:
        pl.semaphore_signal(barrier, inc=1, device_id=tp_at(a, b, d), device_id_type=MESH)

    loads = [
        (q_hbm, qbuf.at[0, pl.ds(0, heads)]),
        (sk_hbm, skbuf),
        (sv_hbm, svbuf),
        (nk_hbm, nkbuf),
        (nv_hbm, nvbuf),
        (pt_hbm, ptbuf),
        (pk_hbm, kbuf.at[0]),
        (pv_hbm, vbuf.at[0]),
        (w_hbm, wbuf.at[0]),
    ]
    loads = [pltpu.make_async_copy(src, dst, local_sem.at[i]) for i, (src, dst) in enumerate(loads)]
    for load in loads:
        load.start()
    for load in loads[:6]:
        load.wait()

    own_q = qbuf[0, :heads]
    slots = skbuf.shape[0]
    scores = lax.dot_general(
        own_q, skbuf[...], (((1,), (1,)), ((), ())), preferred_element_type=jnp.float32
    )
    live = lax.broadcasted_iota(jnp.int32, (heads, slots), 1) < len_ref[0]
    scores = jnp.where(live, scores, -1e30)
    new_score = jnp.sum(
        own_q.astype(jnp.float32) * nkbuf[...].astype(jnp.float32), axis=1, keepdims=True
    )
    suf_max = jnp.maximum(jnp.max(scores, axis=1, keepdims=True), new_score)
    weights = jnp.exp2((scores - suf_max) * scale)
    new_weight = jnp.exp2((new_score - suf_max) * scale)
    suf_mass = jnp.sum(weights, axis=1, keepdims=True) + new_weight
    suf_acc = jnp.dot(weights.astype(jnp.bfloat16), svbuf[...], preferred_element_type=jnp.float32)
    suf_acc = suf_acc + new_weight.astype(jnp.bfloat16).astype(jnp.float32) * nvbuf[...].astype(
        jnp.float32
    )
    suf_max = suf_max * scale

    pages = tokens // 128
    bias = []
    for half in range(2):
        first = (wide - c + (c + half) % 2) * pages
        for page in range(pages):
            used = jnp.max((ptbuf[...] == first + page).astype(jnp.float32), axis=1, keepdims=True)
            bias.append(jnp.broadcast_to((used - 1.0) * 1e30, (1, 128)))
    bias = jnp.concatenate(bias, axis=1)

    for load in loads[6:]:
        load.wait()
    ktbuf[:, :tokens] = kbuf[0].T

    pl.semaphore_wait(barrier, len(WIDE) + len(TP))

    for a, b in WIDE:
        pltpu.make_async_remote_copy(
            qbuf.at[0, pl.ds(0, heads)],
            qbuf.at[a, pl.ds(b * heads, heads)],
            q_send,
            q_recv.at[a],
            device_id=wide_at(a, b),
            device_id_type=MESH,
        ).start()
    swaps = [
        pltpu.make_async_remote_copy(
            buf.at[0],
            buf.at[1],
            core_send.at[i],
            core_recv.at[i],
            device_id=partner,
            device_id_type=MESH,
        )
        for i, buf in enumerate((kbuf, vbuf, wbuf))
    ]
    for swap in swaps:
        swap.start()
    swaps[0].wait_recv()
    ktbuf[:, tokens:] = kbuf[1].T
    swaps[1].wait_recv()
    values = vbuf[...].reshape(2 * tokens, hd)

    def landed(ref, sem):
        pltpu.make_async_copy(ref, ref, sem).wait()

    lane = lax.broadcasted_iota(jnp.int32, (rows, 128), 1)
    for a in (0, 1, 3, 2):
        landed(qbuf.at[0, pl.ds(heads, rows - heads)] if a == 0 else qbuf.at[a], q_recv.at[a])
        s = jnp.dot(qbuf[a], ktbuf[...], preferred_element_type=jnp.float32) + bias
        top = jnp.max(s, axis=1, keepdims=True)
        p = jnp.exp2((s - top) * scale)
        mass = jnp.sum(p, axis=1, keepdims=True)
        acc = jnp.dot(p.astype(jnp.bfloat16), values, preferred_element_type=jnp.float32)
        acc_out[a] = acc.astype(jnp.bfloat16)
        stats = jnp.where(lane == 0, top * scale, jnp.where(lane == 1, mass, 0.0))
        st_out[a] = stats.T[:2]
        for b in (4, 3, 5, 2, 6, 1, 7, 0):
            if (a, b) == (0, 0):
                continue
            pltpu.make_async_remote_copy(
                st_out.at[a],
                st_in.at[a, b],
                st_send,
                st_recv.at[a],
                device_id=wide_at(a, b, -1),
                device_id_type=MESH,
            ).start()
            pltpu.make_async_remote_copy(
                acc_out.at[a, pl.ds(b * heads, heads)],
                acc_in.at[a, pl.ds(b * heads, heads)],
                acc_send,
                acc_recv.at[a],
                device_id=wide_at(a, b, -1),
                device_id_type=MESH,
            ).start()
        if a == 0:
            acc_in[0, :heads] = acc_out[0, :heads]
            st_in[0, 0] = st_out[0]

    spot = lax.broadcasted_iota(jnp.int32, (2, rows), 1) // heads
    joined = []
    for a in range(NY):
        landed(st_in.at[0, pl.ds(1, NZ - 1)] if a == 0 else st_in.at[a], st_recv.at[a])
        line = jnp.zeros((2, rows), jnp.float32)
        for b in range(NZ):
            line = jnp.where(spot == b, st_in[a, b], line)
        joined.append(line)
    tops = jnp.concatenate([line[:1] for line in joined], axis=0)
    masses = jnp.concatenate([line[1:] for line in joined], axis=0)
    best = jnp.broadcast_to(jnp.max(tops, axis=0, keepdims=True), (8, rows))
    for shift in (heads, 2 * heads, 4 * heads):
        best = jnp.maximum(best, pltpu.roll(best, shift, 1))
    factors = jnp.exp2(tops - best[:1])
    mass_line = jnp.sum(factors * masses, axis=0, keepdims=True)
    mine = lax.broadcasted_iota(jnp.int32, (heads, rows), 1) % heads == lax.broadcasted_iota(
        jnp.int32, (heads, rows), 0
    )
    pre_max = jnp.max(jnp.where(mine, best[:1], -3e38), axis=1, keepdims=True)
    pre_mass = jnp.sum(jnp.where(mine, mass_line, 0.0), axis=1, keepdims=True)
    pre_acc = jnp.zeros((2 * heads, hd), jnp.float32)
    for a in range(NY):
        spread = jnp.where(mine, factors[a : a + 1], 0.0)
        high = spread.astype(jnp.bfloat16)
        rest = (spread - high.astype(jnp.float32)).astype(jnp.bfloat16)
        landed(acc_in.at[0, pl.ds(heads, rows - heads)] if a == 0 else acc_in.at[a], acc_recv.at[a])
        pre_acc = pre_acc + jnp.dot(
            jnp.concatenate([high, rest], axis=0), acc_in[a], preferred_element_type=jnp.float32
        )
    row_max = jnp.maximum(pre_max, suf_max)
    pre_factor = jnp.exp2(pre_max - row_max)
    suf_factor = jnp.exp2(suf_max - row_max)
    total = pre_mass * pre_factor + suf_mass * suf_factor
    summed = (pre_acc[:heads] + pre_acc[heads:]) * pre_factor + suf_acc * suf_factor
    own_rows = pl.ds(pl.multiple_of((y * NZ + z) * heads, heads), heads)
    attn_buf[own_rows, :] = (summed / total).astype(jnp.bfloat16)

    for a, b in WIDE:
        pltpu.make_async_remote_copy(
            attn_buf.at[own_rows],
            attn_buf.at[own_rows],
            attn_send,
            attn_recv,
            device_id=wide_at(a, b),
            device_id_type=MESH,
        ).start()
    swaps[2].wait_recv()
    landed(attn_buf.at[pl.ds(0, (CHIPS - 1) * heads)], attn_recv)

    attn32[...] = attn_buf[...].astype(jnp.float32)
    columns = w_hbm.shape[1]
    sums = [jnp.zeros((CHIPS, columns), jnp.float32) for _ in range(2)]
    for h in range(0, heads, 2):
        pair = jnp.concatenate(
            [attn32[pl.ds(h + i, CHIPS, stride=heads), :] for i in range(2)], axis=1
        ).astype(jnp.bfloat16)
        for d in range(2):
            sums[d] = sums[d] + jnp.dot(
                pair, wbuf[d, h * hd : (h + 2) * hd, :], preferred_element_type=jnp.float32
            )
    share = CHIPS // (NX * NL)
    for d in range(2):
        for t in range(NX * NL):
            part = sums[d][t * share : (t + 1) * share]
            proj_out[d, t] = jnp.concatenate([part[:, :128], part[:, 128:]], axis=0)
    for i, (a, b, d) in enumerate(TP):
        target = tp_at(a, b, d)
        pltpu.make_async_remote_copy(
            proj_out.at[d, target[1]],
            proj_in.at[i],
            proj_send,
            proj_recv,
            device_id=target,
            device_id_type=MESH,
        ).start()
    landed(proj_in, proj_recv)
    parts = [proj_out[0, tp], jnp.zeros((8, 128), jnp.float32)]
    for i, (a, b, d) in enumerate(TP):
        parts[d] = parts[d] + proj_in[i]
    for core in range(2):
        half = jnp.where(c == core, parts[0], parts[1])
        for i in range(share):
            for j in range(2):
                o_ref[2 * i + core : 2 * i + core + 1, j * 128 : (j + 1) * 128] = half[
                    j * share + i : j * share + i + 1
                ]

    landed(qbuf.at[pl.ds(0, NY - 1)], q_send)
    landed(qbuf.at[0, pl.ds(heads, rows - heads)], q_send)
    for swap in swaps:
        swap.wait_send()
    landed(acc_out.at[pl.ds(0, NY - 1)], acc_send)
    landed(acc_out.at[0, pl.ds(heads, rows - heads)], acc_send)
    landed(st_in.at[pl.ds(0, NY - 1)], st_send)
    landed(st_in.at[0, pl.ds(1, NZ - 1)], st_send)
    landed(attn_buf.at[pl.ds(0, (CHIPS - 1) * heads)], attn_send)
    landed(proj_in, proj_send)


def local(
    queries,
    new_keys,
    new_values,
    prefix_keys,
    prefix_values,
    suffix_keys,
    suffix_values,
    lengths,
    page_table,
    out_weight,
):
    _, heads, hd = queries.shape
    tokens = prefix_keys.shape[0] * prefix_keys.shape[1]
    slots = suffix_keys.shape[1]
    depth, columns = out_weight.shape
    rows = NZ * heads
    bf16, f32 = jnp.bfloat16, jnp.float32
    dma = pltpu.SemaphoreType.DMA
    return pl.pallas_call(
        kernel,
        out_shape=pltpu.VMEM((8, columns), f32),
        in_specs=[pl.BlockSpec(memory_space=pltpu.SMEM)] + [pl.BlockSpec(memory_space=pl.ANY)] * 9,
        out_specs=pl.BlockSpec(memory_space=pltpu.VMEM),
        scratch_shapes=[
            pltpu.VMEM((NY, rows, hd), bf16),
            pltpu.VMEM((2, tokens, hd), bf16),
            pltpu.VMEM((2, tokens, hd), bf16),
            pltpu.VMEM((hd, 2 * tokens), bf16),
            pltpu.VMEM((slots, hd), bf16),
            pltpu.VMEM((slots, hd), bf16),
            pltpu.VMEM((1, hd), bf16),
            pltpu.VMEM((1, hd), bf16),
            pltpu.VMEM((1, page_table.shape[0]), jnp.int32),
            pltpu.VMEM((2, depth, columns), bf16),
            pltpu.VMEM((NY, rows, hd), bf16),
            pltpu.VMEM((NY, 2, rows), f32),
            pltpu.VMEM((NY, rows, hd), bf16),
            pltpu.VMEM((NY, NZ, 2, rows), f32),
            pltpu.VMEM((CHIPS * heads, hd), bf16),
            pltpu.VMEM((CHIPS * heads, hd), f32),
            pltpu.VMEM((2, NX * NL, 8, 128), f32),
            pltpu.VMEM((len(TP), 8, 128), f32),
            dma((9,)),
            dma,
            dma((NY,)),
            dma((3,)),
            dma((3,)),
            dma,
            dma((NY,)),
            dma,
            dma((NY,)),
            dma,
            dma,
            dma,
            dma,
        ],
        compiler_params=pltpu.CompilerParams(
            collective_id=0, has_side_effects=True, vmem_limit_bytes=32 * 1024 * 1024
        ),
        name="attention_step",
    )(
        lengths,
        *(
            pltpu.with_memory_space_constraint(a, pltpu.HBM)
            for a in (
                queries.reshape(heads, hd),
                new_keys.reshape(1, hd),
                new_values.reshape(1, hd),
                prefix_keys.reshape(tokens, hd),
                prefix_values.reshape(tokens, hd),
                suffix_keys.reshape(slots, hd),
                suffix_values.reshape(slots, hd),
                page_table.reshape(1, -1),
                out_weight,
            )
        ),
    )


def solution(mesh):
    in_specs = (
        P("wide", "tp", None),
        P("wide", "tp", None),
        P("wide", "tp", None),
        P("wide", None, "tp", None),
        P("wide", None, "tp", None),
        P("wide", None, "tp", None),
        P("wide", None, "tp", None),
        P("wide"),
        P(),
        P("tp", "wide"),
    )
    out_specs = P("tp", "wide")
    return jax.shard_map(local, mesh=mesh, in_specs=in_specs, out_specs=out_specs, check_vma=False)
```

```python
import functools

import jax
import jax.numpy as jnp
from jax import lax
from jax.experimental import pallas as pl
from jax.experimental.pallas import tpu as pltpu
from jax.sharding import PartitionSpec as P

MESH = pl.DeviceIdType.MESH
NY, NZ = 4, 8
NX, NL = 4, 2
CHIPS = NY * NZ
WIDE = [(a, b) for a in (2, 1, 3, 0) for b in (4, 3, 5, 2, 6, 1, 7, 0) if (a, b) != (0, 0)]
TP = [(a, b, d) for a in (2, 1, 3, 0) for b in (1, 0) for d in (1, 0) if (a, b, d) != (0, 0, 0)]
GROUPS = ((0,), (1, 3), (2,))
LOG2E = 1.4426950408889634


def kernel(
    len_ref,
    q_hbm,
    nk_hbm,
    nv_hbm,
    pk_hbm,
    pv_hbm,
    sk_hbm,
    sv_hbm,
    pt_hbm,
    w_hbm,
    o_ref,
    qbuf,
    kbuf,
    vbuf,
    ktbuf,
    skbuf,
    svbuf,
    nkbuf,
    nvbuf,
    ptbuf,
    wbuf,
    acc_out,
    st_out,
    acc_in,
    st_in,
    attn_buf,
    attn32,
    proj_out,
    proj_in,
    local_sem,
    q_send,
    q_recv,
    core_send,
    core_recv,
    acc_send,
    acc_recv,
    st_send,
    st_recv,
    attn_send,
    attn_recv,
    proj_send,
    proj_recv,
):
    heads, hd = q_hbm.shape
    tokens = pk_hbm.shape[0]
    rows = NZ * heads
    scale = hd ** (-0.5) * LOG2E
    wide = lax.axis_index("wide")
    tp = lax.axis_index("tp")
    y, z, c = wide // (2 * NZ), (wide // 2) % NZ, wide % 2
    x, low = tp // NL, tp % NL

    def wide_at(a, b, sign=1):
        return (((y + sign * a + NY) % NY) * (2 * NZ) + ((z + sign * b + NZ) % NZ) * 2 + c, tp)

    def tp_at(a, b, d):
        return (wide - c + (c + d) % 2, ((x + a) % NX) * NL + (low + b) % NL)

    partner = tp_at(0, 0, 1)

    barrier = pltpu.get_barrier_semaphore()
    for a, b in WIDE:
        pl.semaphore_signal(barrier, inc=1, device_id=wide_at(a, b), device_id_type=MESH)
    for a, b, d in TP:
        pl.semaphore_signal(barrier, inc=1, device_id=tp_at(a, b, d), device_id_type=MESH)

    loads = [
        (q_hbm, qbuf.at[0, pl.ds(0, heads)]),
        (sk_hbm, skbuf),
        (sv_hbm, svbuf),
        (nk_hbm, nkbuf),
        (nv_hbm, nvbuf),
        (pt_hbm, ptbuf),
        (pk_hbm, kbuf.at[0]),
        (pv_hbm, vbuf.at[0, :, pl.ds(0, hd)]),
        (w_hbm, wbuf.at[0]),
    ]
    loads = [pltpu.make_async_copy(src, dst, local_sem.at[i]) for i, (src, dst) in enumerate(loads)]
    for load in loads:
        load.start()
    for load in loads[:6]:
        load.wait()

    own_q = qbuf[0, :heads]
    slots = skbuf.shape[0]
    scores = lax.dot_general(
        own_q, skbuf[...], (((1,), (1,)), ((), ())), preferred_element_type=jnp.float32
    )
    live = lax.broadcasted_iota(jnp.int32, (heads, slots), 1) < len_ref[0]
    scores = jnp.where(live, scores, -1e30)
    new_score = jnp.sum(
        own_q.astype(jnp.float32) * nkbuf[...].astype(jnp.float32), axis=1, keepdims=True
    )
    suf_max = jnp.maximum(jnp.max(scores, axis=1, keepdims=True), new_score)
    weights = jnp.exp2((scores - suf_max) * scale)
    new_weight = jnp.exp2((new_score - suf_max) * scale)
    suf_mass = jnp.sum(weights, axis=1, keepdims=True) + new_weight
    suf_acc = jnp.dot(weights.astype(jnp.bfloat16), svbuf[...], preferred_element_type=jnp.float32)
    suf_acc = suf_acc + new_weight.astype(jnp.bfloat16).astype(jnp.float32) * nvbuf[...].astype(
        jnp.float32
    )
    suf_max = suf_max * scale

    pages = tokens // 128
    bias = []
    for half in range(2):
        first = (wide - c + (c + half) % 2) * pages
        for page in range(pages):
            used = jnp.max((ptbuf[...] == first + page).astype(jnp.float32), axis=1, keepdims=True)
            bias.append(jnp.broadcast_to((used - 1.0) * 1e30, (1, 128)))
    bias = jnp.concatenate(bias, axis=1)

    for load in loads[6:]:
        load.wait()
    ktbuf[:, :tokens] = kbuf[0].T
    vbuf[:, :, hd:] = jnp.ones((2, tokens, hd), jnp.bfloat16)

    pl.semaphore_wait(barrier, len(WIDE) + len(TP))

    for a, b in WIDE:
        pltpu.make_async_remote_copy(
            qbuf.at[0, pl.ds(0, heads)],
            qbuf.at[a, pl.ds(b * heads, heads)],
            q_send,
            q_recv.at[a],
            device_id=wide_at(a, b),
            device_id_type=MESH,
        ).start()
    swaps = [
        pltpu.make_async_remote_copy(
            src,
            dst,
            core_send.at[i],
            core_recv.at[i],
            device_id=partner,
            device_id_type=MESH,
        )
        for i, (src, dst) in enumerate(
            (
                (kbuf.at[0], kbuf.at[1]),
                (vbuf.at[0, :, pl.ds(0, hd)], vbuf.at[1, :, pl.ds(0, hd)]),
                (wbuf.at[0], wbuf.at[1]),
            )
        )
    ]
    for swap in swaps:
        swap.start()
    swaps[0].wait_recv()
    ktbuf[:, tokens:] = kbuf[1].T
    swaps[1].wait_recv()
    values = vbuf[...].reshape(2 * tokens, 2 * hd)

    def landed(ref, sem):
        pltpu.make_async_copy(ref, ref, sem).wait()

    diagonal = lax.broadcasted_iota(jnp.int32, (rows, 128), 0) == lax.broadcasted_iota(
        jnp.int32, (rows, 128), 1
    )

    def line(column):
        return jnp.sum(jnp.where(diagonal, column, 0.0), axis=0, keepdims=True)

    def chunk(a):
        s = jnp.dot(qbuf[a], ktbuf[...], preferred_element_type=jnp.float32) + bias
        top = jnp.max(s, axis=1, keepdims=True)
        p = jnp.exp2((s - top) * scale).astype(jnp.bfloat16)
        acc = jnp.dot(p, values, preferred_element_type=jnp.float32)
        acc_out[a] = acc[:, :hd].astype(jnp.bfloat16)
        st_out[a] = jnp.concatenate([line(top * scale), line(acc[:, hd:])], axis=0)

    def reply(a):
        for b in (4, 3, 5, 2, 6, 1, 7, 0):
            if (a, b) == (0, 0):
                continue
            pltpu.make_async_remote_copy(
                st_out.at[a],
                st_in.at[a, b],
                st_send,
                st_recv.at[a],
                device_id=wide_at(a, b, -1),
                device_id_type=MESH,
            ).start()
            pltpu.make_async_remote_copy(
                acc_out.at[a, pl.ds(b * heads, heads)],
                acc_in.at[a, pl.ds(b * heads, heads)],
                acc_send,
                acc_recv.at[a],
                device_id=wide_at(a, b, -1),
                device_id_type=MESH,
            ).start()
        if a == 0:
            acc_in[0, :heads] = acc_out[0, :heads]
            st_in[0, 0] = st_out[0]

    for group in GROUPS:
        for a in group:
            landed(qbuf.at[0, pl.ds(heads, rows - heads)] if a == 0 else qbuf.at[a], q_recv.at[a])
        for a in group:
            chunk(a)
        for a in group:
            reply(a)

    spot = lax.broadcasted_iota(jnp.int32, (2, rows), 1) // heads
    joined = []
    for a in range(NY):
        landed(st_in.at[0, pl.ds(1, NZ - 1)] if a == 0 else st_in.at[a], st_recv.at[a])
        both = st_in[a, 0]
        for b in range(1, NZ):
            both = jnp.where(spot == b, st_in[a, b], both)
        joined.append(both)
    best = functools.reduce(jnp.maximum, [both[:1] for both in joined])
    mine = lax.broadcasted_iota(jnp.int32, (heads, rows), 1) % heads == lax.broadcasted_iota(
        jnp.int32, (heads, rows), 0
    )
    row_max = jnp.maximum(
        jnp.max(jnp.where(mine, best, -3e38), axis=1, keepdims=True), suf_max
    )
    spread = [jnp.where(mine, jnp.exp2(both[:1] - row_max), 0.0) for both in joined]
    shares = functools.reduce(jnp.add, [f * both[1:] for f, both in zip(spread, joined)])
    suf_factor = jnp.exp2(suf_max - row_max)
    total = jnp.sum(shares, axis=1, keepdims=True) + suf_mass * suf_factor
    spread = jnp.concatenate(spread, axis=1)
    high = spread.astype(jnp.bfloat16)
    rest = (spread - high.astype(jnp.float32)).astype(jnp.bfloat16)
    factors = jnp.concatenate([high, rest], axis=0)
    for a in range(NY):
        landed(acc_in.at[0, pl.ds(heads, rows - heads)] if a == 0 else acc_in.at[a], acc_recv.at[a])
    pre_acc = jnp.dot(
        factors, acc_in[...].reshape(NY * rows, hd), preferred_element_type=jnp.float32
    )
    summed = pre_acc[:heads] + pre_acc[heads:] + suf_acc * suf_factor
    own_rows = pl.ds(pl.multiple_of((y * NZ + z) * heads, heads), heads)
    attn_buf[own_rows, :] = (summed / total).astype(jnp.bfloat16)

    for a, b in WIDE:
        pltpu.make_async_remote_copy(
            attn_buf.at[own_rows],
            attn_buf.at[own_rows],
            attn_send,
            attn_recv.at[a],
            device_id=wide_at(a, b),
            device_id_type=MESH,
        ).start()
    swaps[2].wait_recv()
    for a in (0, 1, 3, 2):
        block = pl.ds(pl.multiple_of((y - a + NY) % NY * rows, rows), rows)
        landed(attn_buf.at[pl.ds(0, rows - heads if a == 0 else rows)], attn_recv.at[a])
        attn32[block, :] = attn_buf[block, :].astype(jnp.float32)

    columns = w_hbm.shape[1]
    sums = [jnp.zeros((CHIPS, columns), jnp.float32) for _ in range(2)]
    for h in range(0, heads, 2):
        pair = jnp.concatenate(
            [attn32[pl.ds(h + i, CHIPS, stride=heads), :] for i in range(2)], axis=1
        ).astype(jnp.bfloat16)
        for d in range(2):
            sums[d] = sums[d] + jnp.dot(
                pair, wbuf[d, h * hd : (h + 2) * hd, :], preferred_element_type=jnp.float32
            )
    share = CHIPS // (NX * NL)
    for d in range(2):
        for t in range(NX * NL):
            part = sums[d][t * share : (t + 1) * share]
            proj_out[d, t] = jnp.concatenate([part[:, :128], part[:, 128:]], axis=0)
    for i, (a, b, d) in enumerate(TP):
        target = tp_at(a, b, d)
        pltpu.make_async_remote_copy(
            proj_out.at[d, target[1]],
            proj_in.at[i],
            proj_send,
            proj_recv,
            device_id=target,
            device_id_type=MESH,
        ).start()
    landed(proj_in, proj_recv)
    parts = [proj_out[0, tp], jnp.zeros((8, 128), jnp.float32)]
    for i, (a, b, d) in enumerate(TP):
        parts[d] = parts[d] + proj_in[i]
    for core in range(2):
        half = jnp.where(c == core, parts[0], parts[1])
        for i in range(share):
            for j in range(2):
                o_ref[2 * i + core : 2 * i + core + 1, j * 128 : (j + 1) * 128] = half[
                    j * share + i : j * share + i + 1
                ]

    landed(qbuf.at[pl.ds(0, NY - 1)], q_send)
    landed(qbuf.at[0, pl.ds(heads, rows - heads)], q_send)
    for swap in swaps:
        swap.wait_send()
    landed(acc_out.at[pl.ds(0, NY - 1)], acc_send)
    landed(acc_out.at[0, pl.ds(heads, rows - heads)], acc_send)
    landed(st_in.at[pl.ds(0, NY - 1)], st_send)
    landed(st_in.at[0, pl.ds(1, NZ - 1)], st_send)
    landed(attn_buf.at[pl.ds(0, (CHIPS - 1) * heads)], attn_send)
    landed(proj_in, proj_send)


def local(
    queries,
    new_keys,
    new_values,
    prefix_keys,
    prefix_values,
    suffix_keys,
    suffix_values,
    lengths,
    page_table,
    out_weight,
):
    _, heads, hd = queries.shape
    tokens = prefix_keys.shape[0] * prefix_keys.shape[1]
    slots = suffix_keys.shape[1]
    depth, columns = out_weight.shape
    rows = NZ * heads
    bf16, f32 = jnp.bfloat16, jnp.float32
    dma = pltpu.SemaphoreType.DMA
    return pl.pallas_call(
        kernel,
        out_shape=pltpu.VMEM((8, columns), f32),
        in_specs=[pl.BlockSpec(memory_space=pltpu.SMEM)] + [pl.BlockSpec(memory_space=pl.ANY)] * 9,
        out_specs=pl.BlockSpec(memory_space=pltpu.VMEM),
        scratch_shapes=[
            pltpu.VMEM((NY, rows, hd), bf16),
            pltpu.VMEM((2, tokens, hd), bf16),
            pltpu.VMEM((2, tokens, 2 * hd), bf16),
            pltpu.VMEM((hd, 2 * tokens), bf16),
            pltpu.VMEM((slots, hd), bf16),
            pltpu.VMEM((slots, hd), bf16),
            pltpu.VMEM((1, hd), bf16),
            pltpu.VMEM((1, hd), bf16),
            pltpu.VMEM((1, page_table.shape[0]), jnp.int32),
            pltpu.VMEM((2, depth, columns), bf16),
            pltpu.VMEM((NY, rows, hd), bf16),
            pltpu.VMEM((NY, 2, rows), f32),
            pltpu.VMEM((NY, rows, hd), bf16),
            pltpu.VMEM((NY, NZ, 2, rows), f32),
            pltpu.VMEM((CHIPS * heads, hd), bf16),
            pltpu.VMEM((CHIPS * heads, hd), f32),
            pltpu.VMEM((2, NX * NL, 8, 128), f32),
            pltpu.VMEM((len(TP), 8, 128), f32),
            dma((9,)),
            dma,
            dma((NY,)),
            dma((3,)),
            dma((3,)),
            dma,
            dma((NY,)),
            dma,
            dma((NY,)),
            dma,
            dma((NY,)),
            dma,
            dma,
        ],
        compiler_params=pltpu.CompilerParams(
            collective_id=0, has_side_effects=True, vmem_limit_bytes=32 * 1024 * 1024
        ),
        name="attention_step",
    )(
        lengths,
        *(
            pltpu.with_memory_space_constraint(a, pltpu.HBM)
            for a in (
                queries.reshape(heads, hd),
                new_keys.reshape(1, hd),
                new_values.reshape(1, hd),
                prefix_keys.reshape(tokens, hd),
                prefix_values.reshape(tokens, hd),
                suffix_keys.reshape(slots, hd),
                suffix_values.reshape(slots, hd),
                page_table.reshape(1, -1),
                out_weight,
            )
        ),
    )


def solution(mesh):
    in_specs = (
        P("wide", "tp", None),
        P("wide", "tp", None),
        P("wide", "tp", None),
        P("wide", None, "tp", None),
        P("wide", None, "tp", None),
        P("wide", None, "tp", None),
        P("wide", None, "tp", None),
        P("wide"),
        P(),
        P("tp", "wide"),
    )
    out_specs = P("tp", "wide")
    return jax.shard_map(local, mesh=mesh, in_specs=in_specs, out_specs=out_specs, check_vma=False)
```

```python
import functools

import jax
import jax.numpy as jnp
from jax import lax
from jax.experimental import pallas as pl
from jax.experimental.pallas import tpu as pltpu
from jax.sharding import PartitionSpec as P

MESH = pl.DeviceIdType.MESH
NY, NZ = 4, 8
NX, NL = 4, 2
CHIPS = NY * NZ
WIDE = [(a, b) for a in (2, 1, 3, 0) for b in (4, 3, 5, 2, 6, 1, 7, 0) if (a, b) != (0, 0)]
TP = [(a, b, d) for a in (2, 1, 3, 0) for b in (1, 0) for d in (1, 0) if (a, b, d) != (0, 0, 0)]
GROUPS = ((0,), (1, 3), (2,))
LOG2E = 1.4426950408889634


def kernel(
    len_ref,
    q_hbm,
    nk_hbm,
    nv_hbm,
    pk_hbm,
    pv_hbm,
    sk_hbm,
    sv_hbm,
    pt_hbm,
    w_hbm,
    o_ref,
    qbuf,
    kbuf,
    vbuf,
    ktbuf,
    skbuf,
    svbuf,
    nkbuf,
    nvbuf,
    ptbuf,
    wbuf,
    acc_out,
    st_out,
    acc_in,
    st_in,
    attn_buf,
    attn32,
    proj_out,
    proj_in,
    local_sem,
    q_send,
    q_recv,
    core_send,
    core_recv,
    acc_send,
    acc_recv,
    st_send,
    st_recv,
    attn_send,
    attn_recv,
    proj_send,
    proj_recv,
):
    heads, hd = q_hbm.shape
    tokens = pk_hbm.shape[0]
    rows = NZ * heads
    scale = hd ** (-0.5) * LOG2E
    wide = lax.axis_index("wide")
    tp = lax.axis_index("tp")
    y, z, c = wide // (2 * NZ), (wide // 2) % NZ, wide % 2
    x, low = tp // NL, tp % NL

    def wide_at(a, b, sign=1):
        return (((y + sign * a + NY) % NY) * (2 * NZ) + ((z + sign * b + NZ) % NZ) * 2 + c, tp)

    def tp_at(a, b, d):
        return (wide - c + (c + d) % 2, ((x + a) % NX) * NL + (low + b) % NL)

    partner = tp_at(0, 0, 1)

    barrier = pltpu.get_barrier_semaphore()
    for a, b in WIDE:
        pl.semaphore_signal(barrier, inc=1, device_id=wide_at(a, b), device_id_type=MESH)
    for a, b, d in TP:
        pl.semaphore_signal(barrier, inc=1, device_id=tp_at(a, b, d), device_id_type=MESH)

    loads = [
        (q_hbm, qbuf.at[0, pl.ds(0, heads)]),
        (sk_hbm, skbuf),
        (sv_hbm, svbuf),
        (nk_hbm, nkbuf),
        (nv_hbm, nvbuf),
        (pt_hbm, ptbuf),
        (pk_hbm, kbuf.at[0]),
        (pv_hbm, vbuf.at[0, :, pl.ds(0, hd)]),
        (w_hbm, wbuf.at[0]),
    ]
    loads = [pltpu.make_async_copy(src, dst, local_sem.at[i]) for i, (src, dst) in enumerate(loads)]
    for load in loads:
        load.start()
    for load in loads[:6]:
        load.wait()

    own_q = qbuf[0, :heads]
    slots = skbuf.shape[0]
    scores = lax.dot_general(
        own_q, skbuf[...], (((1,), (1,)), ((), ())), preferred_element_type=jnp.float32
    )
    live = lax.broadcasted_iota(jnp.int32, (heads, slots), 1) < len_ref[0]
    scores = jnp.where(live, scores, -1e30)
    new_score = jnp.sum(
        own_q.astype(jnp.float32) * nkbuf[...].astype(jnp.float32), axis=1, keepdims=True
    )
    suf_max = jnp.maximum(jnp.max(scores, axis=1, keepdims=True), new_score)
    weights = jnp.exp2((scores - suf_max) * scale)
    new_weight = jnp.exp2((new_score - suf_max) * scale)
    suf_mass = jnp.sum(weights, axis=1, keepdims=True) + new_weight
    suf_acc = jnp.dot(weights.astype(jnp.bfloat16), svbuf[...], preferred_element_type=jnp.float32)
    suf_acc = suf_acc + new_weight.astype(jnp.bfloat16).astype(jnp.float32) * nvbuf[...].astype(
        jnp.float32
    )
    suf_max = suf_max * scale

    pages = tokens // 128
    bias = []
    for half in range(2):
        first = (wide - c + (c + half) % 2) * pages
        for page in range(pages):
            used = jnp.max((ptbuf[...] == first + page).astype(jnp.float32), axis=1, keepdims=True)
            bias.append(jnp.broadcast_to((used - 1.0) * 1e30, (1, 128)))
    bias = jnp.concatenate(bias, axis=1)

    for load in loads[6:]:
        load.wait()
    ktbuf[:, :tokens] = kbuf[0].T
    vbuf[:, :, hd:] = jnp.ones((2, tokens, hd), jnp.bfloat16)

    pl.semaphore_wait(barrier, len(WIDE) + len(TP))

    for a, b in WIDE:
        pltpu.make_async_remote_copy(
            qbuf.at[0, pl.ds(0, heads)],
            qbuf.at[a, pl.ds(b * heads, heads)],
            q_send,
            q_recv.at[a],
            device_id=wide_at(a, b),
            device_id_type=MESH,
        ).start()
    swaps = [
        pltpu.make_async_remote_copy(
            src,
            dst,
            core_send.at[i],
            core_recv.at[i],
            device_id=partner,
            device_id_type=MESH,
        )
        for i, (src, dst) in enumerate(
            (
                (kbuf.at[0], kbuf.at[1]),
                (vbuf.at[0, :, pl.ds(0, hd)], vbuf.at[1, :, pl.ds(0, hd)]),
                (wbuf.at[0], wbuf.at[1]),
            )
        )
    ]
    for swap in swaps:
        swap.start()
    swaps[0].wait_recv()
    ktbuf[:, tokens:] = kbuf[1].T
    swaps[1].wait_recv()
    values = vbuf[...].reshape(2 * tokens, 2 * hd)

    def landed(ref, sem):
        pltpu.make_async_copy(ref, ref, sem).wait()

    diagonal = lax.broadcasted_iota(jnp.int32, (rows, 128), 0) == lax.broadcasted_iota(
        jnp.int32, (rows, 128), 1
    )

    def line(column):
        return jnp.sum(jnp.where(diagonal, column, 0.0), axis=0, keepdims=True)

    def chunk(a):
        s = jnp.dot(qbuf[a], ktbuf[...], preferred_element_type=jnp.float32) + bias
        top = jnp.max(s, axis=1, keepdims=True)
        p = jnp.exp2((s - top) * scale).astype(jnp.bfloat16)
        acc = jnp.dot(p, values, preferred_element_type=jnp.float32)
        acc_out[a] = acc[:, :hd].astype(jnp.bfloat16)
        st_out[a] = jnp.concatenate([line(top * scale), line(acc[:, hd:])], axis=0)

    def reply(a):
        for b in (4, 3, 5, 2, 6, 1, 7, 0):
            if (a, b) == (0, 0):
                continue
            pltpu.make_async_remote_copy(
                st_out.at[a],
                st_in.at[a, b],
                st_send,
                st_recv.at[a],
                device_id=wide_at(a, b, -1),
                device_id_type=MESH,
            ).start()
            pltpu.make_async_remote_copy(
                acc_out.at[a, pl.ds(b * heads, heads)],
                acc_in.at[a, pl.ds(b * heads, heads)],
                acc_send,
                acc_recv.at[a],
                device_id=wide_at(a, b, -1),
                device_id_type=MESH,
            ).start()
        if a == 0:
            acc_in[0, :heads] = acc_out[0, :heads]
            st_in[0, 0] = st_out[0]

    for group in GROUPS:
        for a in group:
            landed(qbuf.at[0, pl.ds(heads, rows - heads)] if a == 0 else qbuf.at[a], q_recv.at[a])
        for a in group:
            chunk(a)
        for a in group:
            reply(a)

    spot = lax.broadcasted_iota(jnp.int32, (2, rows), 1) // heads
    joined = []
    for a in range(NY):
        landed(st_in.at[0, pl.ds(1, NZ - 1)] if a == 0 else st_in.at[a], st_recv.at[a])
        both = st_in[a, 0]
        for b in range(1, NZ):
            both = jnp.where(spot == b, st_in[a, b], both)
        joined.append(both)
    best = functools.reduce(jnp.maximum, [both[:1] for both in joined])
    mine = lax.broadcasted_iota(jnp.int32, (heads, rows), 1) % heads == lax.broadcasted_iota(
        jnp.int32, (heads, rows), 0
    )
    row_max = jnp.maximum(
        jnp.max(jnp.where(mine, best, -3e38), axis=1, keepdims=True), suf_max
    )
    spread = [jnp.where(mine, jnp.exp2(both[:1] - row_max), 0.0) for both in joined]
    shares = functools.reduce(jnp.add, [f * both[1:] for f, both in zip(spread, joined)])
    suf_factor = jnp.exp2(suf_max - row_max)
    total = jnp.sum(shares, axis=1, keepdims=True) + suf_mass * suf_factor
    spread = jnp.concatenate(spread, axis=1)
    high = spread.astype(jnp.bfloat16)
    rest = (spread - high.astype(jnp.float32)).astype(jnp.bfloat16)
    factors = jnp.concatenate([high, rest], axis=0)
    for a in range(NY):
        landed(acc_in.at[0, pl.ds(heads, rows - heads)] if a == 0 else acc_in.at[a], acc_recv.at[a])
    pre_acc = jnp.dot(
        factors, acc_in[...].reshape(NY * rows, hd), preferred_element_type=jnp.float32
    )
    summed = pre_acc[:heads] + pre_acc[heads:] + suf_acc * suf_factor
    own_rows = pl.ds(pl.multiple_of((y * NZ + z) * heads, heads), heads)
    attn_buf[own_rows, :] = (summed / total).astype(jnp.bfloat16)

    for a, b in WIDE:
        pltpu.make_async_remote_copy(
            attn_buf.at[own_rows],
            attn_buf.at[own_rows],
            attn_send,
            attn_recv.at[y],
            device_id=wide_at(a, b),
            device_id_type=MESH,
        ).start()
    swaps[2].wait_recv()
    def rows_of(plane):
        sem = attn_recv.at[plane]
        pl.when(y == plane)(lambda: landed(attn_buf.at[pl.ds(0, rows - heads)], sem))
        pl.when(y != plane)(lambda: landed(attn_buf.at[pl.ds(0, rows)], sem))
        block = slice(plane * rows, (plane + 1) * rows)
        attn32[block, :] = attn_buf[block, :].astype(jnp.float32)

    columns = w_hbm.shape[1]
    share = CHIPS // (NX * NL)

    def project(first, count):
        sums = [jnp.zeros((count, columns), jnp.float32) for _ in range(2)]
        for h in range(0, heads, 2):
            pair = jnp.concatenate(
                [
                    attn32[pl.ds(first * heads + h + i, count, stride=heads), :]
                    for i in range(2)
                ],
                axis=1,
            ).astype(jnp.bfloat16)
            for d in range(2):
                sums[d] = sums[d] + jnp.dot(
                    pair, wbuf[d, h * hd : (h + 2) * hd, :], preferred_element_type=jnp.float32
                )
        for d in range(2):
            for t in range(count // share):
                part = sums[d][t * share : (t + 1) * share]
                proj_out[d, first // share + t] = jnp.concatenate(
                    [part[:, :128], part[:, 128:]], axis=0
                )

    def send_sums(wanted):
        for i, (a, b, d) in enumerate(TP):
            target = tp_at(a, b, d)
            copy = pltpu.make_async_remote_copy(
                proj_out.at[d, target[1]],
                proj_in.at[i],
                proj_send,
                proj_recv,
                device_id=target,
                device_id_type=MESH,
            )
            pl.when(wanted((x + a) % NX))(copy.start)

    rows_of(0)
    project(0, NZ)
    send_sums(lambda to: to == 0)
    for plane in range(1, NY):
        rows_of(plane)
    project(NZ, CHIPS - NZ)
    send_sums(lambda to: to != 0)
    landed(proj_in, proj_recv)
    parts = [proj_out[0, tp], jnp.zeros((8, 128), jnp.float32)]
    for i, (a, b, d) in enumerate(TP):
        parts[d] = parts[d] + proj_in[i]
    for core in range(2):
        half = jnp.where(c == core, parts[0], parts[1])
        for i in range(share):
            for j in range(2):
                o_ref[2 * i + core : 2 * i + core + 1, j * 128 : (j + 1) * 128] = half[
                    j * share + i : j * share + i + 1
                ]

    landed(qbuf.at[pl.ds(0, NY - 1)], q_send)
    landed(qbuf.at[0, pl.ds(heads, rows - heads)], q_send)
    for swap in swaps:
        swap.wait_send()
    landed(acc_out.at[pl.ds(0, NY - 1)], acc_send)
    landed(acc_out.at[0, pl.ds(heads, rows - heads)], acc_send)
    landed(st_in.at[pl.ds(0, NY - 1)], st_send)
    landed(st_in.at[0, pl.ds(1, NZ - 1)], st_send)
    landed(attn_buf.at[pl.ds(0, (CHIPS - 1) * heads)], attn_send)
    landed(proj_in, proj_send)


def local(
    queries,
    new_keys,
    new_values,
    prefix_keys,
    prefix_values,
    suffix_keys,
    suffix_values,
    lengths,
    page_table,
    out_weight,
):
    _, heads, hd = queries.shape
    tokens = prefix_keys.shape[0] * prefix_keys.shape[1]
    slots = suffix_keys.shape[1]
    depth, columns = out_weight.shape
    rows = NZ * heads
    bf16, f32 = jnp.bfloat16, jnp.float32
    dma = pltpu.SemaphoreType.DMA
    return pl.pallas_call(
        kernel,
        out_shape=pltpu.VMEM((8, columns), f32),
        in_specs=[pl.BlockSpec(memory_space=pltpu.SMEM)] + [pl.BlockSpec(memory_space=pl.ANY)] * 9,
        out_specs=pl.BlockSpec(memory_space=pltpu.VMEM),
        scratch_shapes=[
            pltpu.VMEM((NY, rows, hd), bf16),
            pltpu.VMEM((2, tokens, hd), bf16),
            pltpu.VMEM((2, tokens, 2 * hd), bf16),
            pltpu.VMEM((hd, 2 * tokens), bf16),
            pltpu.VMEM((slots, hd), bf16),
            pltpu.VMEM((slots, hd), bf16),
            pltpu.VMEM((1, hd), bf16),
            pltpu.VMEM((1, hd), bf16),
            pltpu.VMEM((1, page_table.shape[0]), jnp.int32),
            pltpu.VMEM((2, depth, columns), bf16),
            pltpu.VMEM((NY, rows, hd), bf16),
            pltpu.VMEM((NY, 2, rows), f32),
            pltpu.VMEM((NY, rows, hd), bf16),
            pltpu.VMEM((NY, NZ, 2, rows), f32),
            pltpu.VMEM((CHIPS * heads, hd), bf16),
            pltpu.VMEM((CHIPS * heads, hd), f32),
            pltpu.VMEM((2, NX * NL, 8, 128), f32),
            pltpu.VMEM((len(TP), 8, 128), f32),
            dma((9,)),
            dma,
            dma((NY,)),
            dma((3,)),
            dma((3,)),
            dma,
            dma((NY,)),
            dma,
            dma((NY,)),
            dma,
            dma((NY,)),
            dma,
            dma,
        ],
        compiler_params=pltpu.CompilerParams(
            collective_id=0, has_side_effects=True, vmem_limit_bytes=32 * 1024 * 1024
        ),
        name="attention_step",
    )(
        lengths,
        *(
            pltpu.with_memory_space_constraint(a, pltpu.HBM)
            for a in (
                queries.reshape(heads, hd),
                new_keys.reshape(1, hd),
                new_values.reshape(1, hd),
                prefix_keys.reshape(tokens, hd),
                prefix_values.reshape(tokens, hd),
                suffix_keys.reshape(slots, hd),
                suffix_values.reshape(slots, hd),
                page_table.reshape(1, -1),
                out_weight,
            )
        ),
    )


def solution(mesh):
    in_specs = (
        P("wide", "tp", None),
        P("wide", "tp", None),
        P("wide", "tp", None),
        P("wide", None, "tp", None),
        P("wide", None, "tp", None),
        P("wide", None, "tp", None),
        P("wide", None, "tp", None),
        P("wide"),
        P(),
        P("tp", "wide"),
    )
    out_specs = P("tp", "wide")
    return jax.shard_map(local, mesh=mesh, in_specs=in_specs, out_specs=out_specs, check_vma=False)
```

```python
import functools

import jax
import jax.numpy as jnp
from jax import lax
from jax.experimental import pallas as pl
from jax.experimental.pallas import tpu as pltpu
from jax.sharding import PartitionSpec as P

MESH = pl.DeviceIdType.MESH
NY, NZ = 4, 8
NX, NL = 4, 2
CHIPS = NY * NZ
WIDE = [(a, b) for a in (2, 1, 3, 0) for b in (4, 3, 5, 2, 6, 1, 7, 0) if (a, b) != (0, 0)]
TP = [(a, b, d) for a in (2, 1, 3, 0) for b in (1, 0) for d in (1, 0) if (a, b, d) != (0, 0, 0)]
GROUPS = ((0,), (1, 3), (2,))
LOG2E = 1.4426950408889634


def kernel(
    len_ref,
    q_hbm,
    nk_hbm,
    nv_hbm,
    pk_hbm,
    pv_hbm,
    sk_hbm,
    sv_hbm,
    pt_hbm,
    w_hbm,
    o_ref,
    qbuf,
    kbuf,
    vbuf,
    ktbuf,
    skbuf,
    svbuf,
    nkbuf,
    nvbuf,
    ptbuf,
    wbuf,
    acc_out,
    st_out,
    acc_in,
    st_in,
    suf_out,
    suf_in,
    attn_buf,
    attn32,
    proj_out,
    proj_in,
    local_sem,
    q_send,
    q_recv,
    core_send,
    core_recv,
    acc_send,
    acc_recv,
    st_send,
    st_recv,
    suf_send,
    suf_recv,
    attn_send,
    attn_recv,
    proj_send,
    proj_recv,
):
    heads, hd = q_hbm.shape
    tokens = pk_hbm.shape[0]
    rows = NZ * heads
    scale = hd ** (-0.5) * LOG2E
    wide = lax.axis_index("wide")
    tp = lax.axis_index("tp")
    y, z, c = wide // (2 * NZ), (wide // 2) % NZ, wide % 2
    x, low = tp // NL, tp % NL

    def wide_at(a, b):
        return (((y + a) % NY) * (2 * NZ) + ((z + b) % NZ) * 2 + c, tp)

    def join_at(a, b):
        of_y, of_z = (y - a + NY) % NY, (z - b + NZ) % NZ
        return (of_z // 2 * (2 * NZ) + (of_y + of_z % 2 * (NZ - 1 - 2 * of_y)) * 2 + c, tp)

    join_y, join_z = z + z // NY * (NZ - 1 - 2 * z), 2 * y + z // NY
    suffix_to = join_at(0, 0)
    moved = suffix_to[0] != wide

    def tp_at(a, b, d):
        return (wide - c + (c + d) % 2, ((x + a) % NX) * NL + (low + b) % NL)

    partner = tp_at(0, 0, 1)

    barrier = pltpu.get_barrier_semaphore()
    for a, b in WIDE:
        pl.semaphore_signal(barrier, inc=1, device_id=wide_at(a, b), device_id_type=MESH)
    for a, b, d in TP:
        pl.semaphore_signal(barrier, inc=1, device_id=tp_at(a, b, d), device_id_type=MESH)

    loads = [
        (q_hbm, qbuf.at[0, pl.ds(0, heads)]),
        (sk_hbm, skbuf),
        (sv_hbm, svbuf),
        (nk_hbm, nkbuf),
        (nv_hbm, nvbuf),
        (pt_hbm, ptbuf),
        (pk_hbm, kbuf.at[0]),
        (pv_hbm, vbuf.at[0, :, pl.ds(0, hd)]),
        (w_hbm, wbuf.at[0]),
    ]
    loads = [pltpu.make_async_copy(src, dst, local_sem.at[i]) for i, (src, dst) in enumerate(loads)]
    for load in loads:
        load.start()
    for load in loads[:6]:
        load.wait()

    own_q = qbuf[0, :heads]
    slots = skbuf.shape[0]
    scores = lax.dot_general(
        own_q, skbuf[...], (((1,), (1,)), ((), ())), preferred_element_type=jnp.float32
    )
    live = lax.broadcasted_iota(jnp.int32, (heads, slots), 1) < len_ref[0]
    scores = jnp.where(live, scores, -1e30)
    new_score = jnp.sum(
        own_q.astype(jnp.float32) * nkbuf[...].astype(jnp.float32), axis=1, keepdims=True
    )
    suf_max = jnp.maximum(jnp.max(scores, axis=1, keepdims=True), new_score)
    weights = jnp.exp2((scores - suf_max) * scale)
    new_weight = jnp.exp2((new_score - suf_max) * scale)
    suf_mass = jnp.sum(weights, axis=1, keepdims=True) + new_weight
    suf_acc = jnp.dot(weights.astype(jnp.bfloat16), svbuf[...], preferred_element_type=jnp.float32)
    suf_acc = suf_acc + new_weight.astype(jnp.bfloat16).astype(jnp.float32) * nvbuf[...].astype(
        jnp.float32
    )
    suf_out[:heads] = suf_acc
    suf_out[heads:] = jnp.where(
        lax.broadcasted_iota(jnp.int32, (heads, hd), 1) == 0, suf_max * scale, suf_mass
    )

    pages = tokens // 128
    bias = []
    for half in range(2):
        first = (wide - c + (c + half) % 2) * pages
        for page in range(pages):
            used = jnp.max((ptbuf[...] == first + page).astype(jnp.float32), axis=1, keepdims=True)
            bias.append(jnp.broadcast_to((used - 1.0) * 1e30, (1, 128)))
    bias = jnp.concatenate(bias, axis=1)

    for load in loads[6:]:
        load.wait()
    ktbuf[:, :tokens] = kbuf[0].T
    vbuf[:, :, hd:] = jnp.ones((2, tokens, hd), jnp.bfloat16)

    pl.semaphore_wait(barrier, len(WIDE) + len(TP))

    for a, b in WIDE:
        pltpu.make_async_remote_copy(
            qbuf.at[0, pl.ds(0, heads)],
            qbuf.at[a, pl.ds(b * heads, heads)],
            q_send,
            q_recv.at[a],
            device_id=wide_at(a, b),
            device_id_type=MESH,
        ).start()
    suffix = pltpu.make_async_remote_copy(
        suf_out,
        suf_in,
        suf_send,
        suf_recv,
        device_id=suffix_to,
        device_id_type=MESH,
    )
    pl.when(moved)(suffix.start)

    @pl.when(jnp.logical_not(moved))
    def _():
        suf_in[...] = suf_out[...]

    swaps = [
        pltpu.make_async_remote_copy(
            src,
            dst,
            core_send.at[i],
            core_recv.at[i],
            device_id=partner,
            device_id_type=MESH,
        )
        for i, (src, dst) in enumerate(
            (
                (kbuf.at[0], kbuf.at[1]),
                (vbuf.at[0, :, pl.ds(0, hd)], vbuf.at[1, :, pl.ds(0, hd)]),
                (wbuf.at[0], wbuf.at[1]),
            )
        )
    ]
    for swap in swaps:
        swap.start()
    swaps[0].wait_recv()
    ktbuf[:, tokens:] = kbuf[1].T
    swaps[1].wait_recv()
    values = vbuf[...].reshape(2 * tokens, 2 * hd)

    def landed(ref, sem):
        pltpu.make_async_copy(ref, ref, sem).wait()

    diagonal = lax.broadcasted_iota(jnp.int32, (rows, 128), 0) == lax.broadcasted_iota(
        jnp.int32, (rows, 128), 1
    )

    def line(column):
        return jnp.sum(jnp.where(diagonal, column, 0.0), axis=0, keepdims=True)

    def chunk(a):
        s = jnp.dot(qbuf[a], ktbuf[...], preferred_element_type=jnp.float32) + bias
        top = jnp.max(s, axis=1, keepdims=True)
        p = jnp.exp2((s - top) * scale).astype(jnp.bfloat16)
        acc = jnp.dot(p, values, preferred_element_type=jnp.float32)
        acc_out[a] = acc[:, :hd].astype(jnp.bfloat16)
        st_out[a] = jnp.concatenate([line(top * scale), line(acc[:, hd:])], axis=0)

    def reply(a):
        for b in (4, 3, 5, 2, 6, 1, 7, 0):
            target = join_at(a, b)
            place = pl.ds(b * heads, heads)
            into = pl.ds((a * NZ + b) * heads, heads)

            @pl.when(target[0] != wide)
            def _():
                pltpu.make_async_remote_copy(
                    st_out.at[a],
                    st_in.at[a * NZ + b],
                    st_send,
                    st_recv,
                    device_id=target,
                    device_id_type=MESH,
                ).start()
                pltpu.make_async_remote_copy(
                    acc_out.at[a, place],
                    acc_in.at[into],
                    acc_send,
                    acc_recv,
                    device_id=target,
                    device_id_type=MESH,
                ).start()

            @pl.when(target[0] == wide)
            def _():
                st_in[a * NZ + b] = st_out[a]
                acc_in[into, :] = acc_out[a, place, :]

    for group in GROUPS:
        for a in group:
            landed(qbuf.at[0, pl.ds(heads, rows - heads)] if a == 0 else qbuf.at[a], q_recv.at[a])
        for a in group:
            chunk(a)
        for a in group:
            reply(a)

    spot = lax.broadcasted_iota(jnp.int32, (2, rows), 1) // heads
    joined = []
    landed(st_in.at[pl.ds(0, CHIPS - 1)], st_recv)
    pl.when(moved)(lambda: landed(suf_in, suf_recv))
    suf_acc, suf_max, suf_mass = suf_in[:heads], suf_in[heads:, :1], suf_in[heads:, 1:2]
    for a in range(NY):
        both = st_in[a * NZ]
        for b in range(1, NZ):
            both = jnp.where(spot == b, st_in[a * NZ + b], both)
        joined.append(both)
    best = functools.reduce(jnp.maximum, [both[:1] for both in joined])
    mine = lax.broadcasted_iota(jnp.int32, (heads, rows), 1) % heads == lax.broadcasted_iota(
        jnp.int32, (heads, rows), 0
    )
    row_max = jnp.maximum(
        jnp.max(jnp.where(mine, best, -3e38), axis=1, keepdims=True), suf_max
    )
    spread = [jnp.where(mine, jnp.exp2(both[:1] - row_max), 0.0) for both in joined]
    shares = functools.reduce(jnp.add, [f * both[1:] for f, both in zip(spread, joined)])
    suf_factor = jnp.exp2(suf_max - row_max)
    total = jnp.sum(shares, axis=1, keepdims=True) + suf_mass * suf_factor
    spread = jnp.concatenate(spread, axis=1)
    high = spread.astype(jnp.bfloat16)
    rest = (spread - high.astype(jnp.float32)).astype(jnp.bfloat16)
    factors = jnp.concatenate([high, rest], axis=0)
    landed(acc_in.at[pl.ds(0, (CHIPS - 1) * heads)], acc_recv)
    pre_acc = jnp.dot(factors, acc_in[...], preferred_element_type=jnp.float32)
    summed = pre_acc[:heads] + pre_acc[heads:] + suf_acc * suf_factor
    own_rows = pl.ds(pl.multiple_of((join_y * NZ + join_z) * heads, heads), heads)
    attn_buf[own_rows, :] = (summed / total).astype(jnp.bfloat16)

    def send_rows(device):
        pltpu.make_async_remote_copy(
            attn_buf.at[own_rows],
            attn_buf.at[own_rows],
            attn_send,
            attn_recv.at[join_y],
            device_id=device,
            device_id_type=MESH,
        ).start()

    for plane in (0, 1, 2, 3, 4, 5, 6, 7):
        for a in (2, 1, 3, 0):
            device = ((y + a) % NY * (2 * NZ) + plane * 2 + c, tp)
            if a:
                send_rows(device)
            else:
                pl.when(z != plane)(functools.partial(send_rows, device))
    swaps[2].wait_recv()
    def rows_of(plane):
        sem = attn_recv.at[plane]
        pl.when(join_y == plane)(lambda: landed(attn_buf.at[pl.ds(0, rows - heads)], sem))
        pl.when(join_y != plane)(lambda: landed(attn_buf.at[pl.ds(0, rows)], sem))
        block = slice(plane * rows, (plane + 1) * rows)
        attn32[block, :] = attn_buf[block, :].astype(jnp.float32)

    columns = w_hbm.shape[1]
    share = CHIPS // (NX * NL)

    def project(first, count):
        sums = [jnp.zeros((count, columns), jnp.float32) for _ in range(2)]
        for h in range(0, heads, 2):
            pair = jnp.concatenate(
                [
                    attn32[pl.ds(first * heads + h + i, count, stride=heads), :]
                    for i in range(2)
                ],
                axis=1,
            ).astype(jnp.bfloat16)
            for d in range(2):
                sums[d] = sums[d] + jnp.dot(
                    pair, wbuf[d, h * hd : (h + 2) * hd, :], preferred_element_type=jnp.float32
                )
        for d in range(2):
            for t in range(count // share):
                part = sums[d][t * share : (t + 1) * share]
                proj_out[d, first // share + t] = jnp.concatenate(
                    [part[:, :128], part[:, 128:]], axis=0
                )

    def send_sums(wanted):
        for i, (a, b, d) in enumerate(TP):
            target = tp_at(a, b, d)
            copy = pltpu.make_async_remote_copy(
                proj_out.at[d, target[1]],
                proj_in.at[i],
                proj_send,
                proj_recv,
                device_id=target,
                device_id_type=MESH,
            )
            pl.when(wanted((x + a) % NX))(copy.start)

    for plane in range(2):
        rows_of(plane)
        project(plane * NZ, NZ)
        send_sums(lambda to: to == plane)
    for plane in range(2, NY):
        rows_of(plane)
    project(2 * NZ, CHIPS - 2 * NZ)
    send_sums(lambda to: to > 1)
    landed(proj_in, proj_recv)
    parts = [proj_out[0, tp], jnp.zeros((8, 128), jnp.float32)]
    for i, (a, b, d) in enumerate(TP):
        parts[d] = parts[d] + proj_in[i]
    for core in range(2):
        half = jnp.where(c == core, parts[0], parts[1])
        for i in range(share):
            for j in range(2):
                o_ref[2 * i + core : 2 * i + core + 1, j * 128 : (j + 1) * 128] = half[
                    j * share + i : j * share + i + 1
                ]

    landed(qbuf.at[pl.ds(0, NY - 1)], q_send)
    landed(qbuf.at[0, pl.ds(heads, rows - heads)], q_send)
    for swap in swaps:
        swap.wait_send()
    landed(acc_out.at[pl.ds(0, NY - 1)], acc_send)
    landed(acc_out.at[0, pl.ds(heads, rows - heads)], acc_send)
    landed(st_in.at[pl.ds(0, CHIPS - 1)], st_send)
    pl.when(moved)(suffix.wait_send)
    landed(attn_buf.at[pl.ds(0, (CHIPS - 1) * heads)], attn_send)
    landed(proj_in, proj_send)


def local(
    queries,
    new_keys,
    new_values,
    prefix_keys,
    prefix_values,
    suffix_keys,
    suffix_values,
    lengths,
    page_table,
    out_weight,
):
    _, heads, hd = queries.shape
    tokens = prefix_keys.shape[0] * prefix_keys.shape[1]
    slots = suffix_keys.shape[1]
    depth, columns = out_weight.shape
    rows = NZ * heads
    bf16, f32 = jnp.bfloat16, jnp.float32
    dma = pltpu.SemaphoreType.DMA
    return pl.pallas_call(
        kernel,
        out_shape=pltpu.VMEM((8, columns), f32),
        in_specs=[pl.BlockSpec(memory_space=pltpu.SMEM)] + [pl.BlockSpec(memory_space=pl.ANY)] * 9,
        out_specs=pl.BlockSpec(memory_space=pltpu.VMEM),
        scratch_shapes=[
            pltpu.VMEM((NY, rows, hd), bf16),
            pltpu.VMEM((2, tokens, hd), bf16),
            pltpu.VMEM((2, tokens, 2 * hd), bf16),
            pltpu.VMEM((hd, 2 * tokens), bf16),
            pltpu.VMEM((slots, hd), bf16),
            pltpu.VMEM((slots, hd), bf16),
            pltpu.VMEM((1, hd), bf16),
            pltpu.VMEM((1, hd), bf16),
            pltpu.VMEM((1, page_table.shape[0]), jnp.int32),
            pltpu.VMEM((2, depth, columns), bf16),
            pltpu.VMEM((NY, rows, hd), bf16),
            pltpu.VMEM((NY, 2, rows), f32),
            pltpu.VMEM((CHIPS * heads, hd), bf16),
            pltpu.VMEM((CHIPS, 2, rows), f32),
            pltpu.VMEM((2 * heads, hd), f32),
            pltpu.VMEM((2 * heads, hd), f32),
            pltpu.VMEM((CHIPS * heads, hd), bf16),
            pltpu.VMEM((CHIPS * heads, hd), f32),
            pltpu.VMEM((2, NX * NL, 8, 128), f32),
            pltpu.VMEM((len(TP), 8, 128), f32),
            dma((9,)),
            dma,
            dma((NY,)),
            dma((3,)),
            dma((3,)),
            dma,
            dma,
            dma,
            dma,
            dma,
            dma,
            dma,
            dma((NY,)),
            dma,
            dma,
        ],
        compiler_params=pltpu.CompilerParams(
            collective_id=0, has_side_effects=True, vmem_limit_bytes=32 * 1024 * 1024
        ),
        name="attention_step",
    )(
        lengths,
        *(
            pltpu.with_memory_space_constraint(a, pltpu.HBM)
            for a in (
                queries.reshape(heads, hd),
                new_keys.reshape(1, hd),
                new_values.reshape(1, hd),
                prefix_keys.reshape(tokens, hd),
                prefix_values.reshape(tokens, hd),
                suffix_keys.reshape(slots, hd),
                suffix_values.reshape(slots, hd),
                page_table.reshape(1, -1),
                out_weight,
            )
        ),
    )


def solution(mesh):
    in_specs = (
        P("wide", "tp", None),
        P("wide", "tp", None),
        P("wide", "tp", None),
        P("wide", None, "tp", None),
        P("wide", None, "tp", None),
        P("wide", None, "tp", None),
        P("wide", None, "tp", None),
        P("wide"),
        P(),
        P("tp", "wide"),
    )
    out_specs = P("tp", "wide")
    return jax.shard_map(local, mesh=mesh, in_specs=in_specs, out_specs=out_specs, check_vma=False)
```

```python
import functools

import jax
import jax.numpy as jnp
from jax import lax
from jax.experimental import pallas as pl
from jax.experimental.pallas import tpu as pltpu
from jax.sharding import PartitionSpec as P

MESH = pl.DeviceIdType.MESH
NY, NZ = 4, 8
NX, NL = 4, 2
CHIPS = NY * NZ
WIDE = [(a, b) for a in (2, 1, 3, 0) for b in (4, 3, 5, 2, 6, 1, 7, 0) if (a, b) != (0, 0)]
TP = [(a, b, d) for a in (2, 1, 3, 0) for b in (1, 0) for d in (1, 0) if (a, b, d) != (0, 0, 0)]
GROUPS = ((0,), (1, 3), (2,))
LOG2E = 1.4426950408889634


def kernel(
    len_ref,
    q_hbm,
    nk_hbm,
    nv_hbm,
    pk_hbm,
    pv_hbm,
    sk_hbm,
    sv_hbm,
    pt_hbm,
    w_hbm,
    o_ref,
    qbuf,
    kbuf,
    vbuf,
    ktbuf,
    skbuf,
    svbuf,
    nkbuf,
    nvbuf,
    ptbuf,
    wbuf,
    acc_out,
    st_out,
    acc_in,
    st_in,
    suf_out,
    suf_in,
    attn_buf,
    attn32,
    proj_out,
    proj_in,
    local_sem,
    q_send,
    q_recv,
    core_send,
    core_recv,
    acc_send,
    acc_recv,
    st_send,
    st_recv,
    suf_send,
    suf_recv,
    attn_send,
    attn_recv,
    proj_send,
    proj_recv,
):
    heads, hd = q_hbm.shape
    tokens = pk_hbm.shape[0]
    rows = NZ * heads
    scale = hd ** (-0.5) * LOG2E
    wide = lax.axis_index("wide")
    tp = lax.axis_index("tp")
    y, z, c = wide // (2 * NZ), (wide // 2) % NZ, wide % 2
    x, low = tp // NL, tp % NL

    def wide_at(a, b):
        return (((y + a) % NY) * (2 * NZ) + ((z + b) % NZ) * 2 + c, tp)

    def join_at(a, b):
        of_y, of_z = (y - a + NY) % NY, (z - b + NZ) % NZ
        return (of_z // 2 * (2 * NZ) + (of_y + of_z % 2 * (NZ - 1 - 2 * of_y)) * 2 + c, tp)

    join_y, join_z = z + z // NY * (NZ - 1 - 2 * z), 2 * y + z // NY
    suffix_to = join_at(0, 0)
    moved = suffix_to[0] != wide

    def tp_at(a, b, d):
        return (wide - c + (c + d) % 2, ((x + a) % NX) * NL + (low + b) % NL)

    partner = tp_at(0, 0, 1)

    barrier = pltpu.get_barrier_semaphore()
    for a, b in WIDE:
        pl.semaphore_signal(barrier, inc=1, device_id=wide_at(a, b), device_id_type=MESH)
    for a, b, d in TP:
        pl.semaphore_signal(barrier, inc=1, device_id=tp_at(a, b, d), device_id_type=MESH)

    loads = [
        (q_hbm, qbuf.at[0, pl.ds(0, heads)]),
        (sk_hbm, skbuf),
        (sv_hbm, svbuf),
        (nk_hbm, nkbuf),
        (nv_hbm, nvbuf),
        (pt_hbm, ptbuf),
        (pk_hbm, kbuf.at[0]),
        (pv_hbm, vbuf.at[0, :, pl.ds(0, hd)]),
        (w_hbm, wbuf.at[0]),
    ]
    loads = [pltpu.make_async_copy(src, dst, local_sem.at[i]) for i, (src, dst) in enumerate(loads)]
    for load in loads:
        load.start()
    for load in loads[:6]:
        load.wait()

    own_q = qbuf[0, :heads]
    slots = skbuf.shape[0]
    scores = lax.dot_general(
        own_q, skbuf[...], (((1,), (1,)), ((), ())), preferred_element_type=jnp.float32
    )
    live = lax.broadcasted_iota(jnp.int32, (heads, slots), 1) < len_ref[0]
    scores = jnp.where(live, scores, -1e30)
    new_score = jnp.sum(
        own_q.astype(jnp.float32) * nkbuf[...].astype(jnp.float32), axis=1, keepdims=True
    )
    suf_max = jnp.maximum(jnp.max(scores, axis=1, keepdims=True), new_score)
    weights = jnp.exp2((scores - suf_max) * scale)
    new_weight = jnp.exp2((new_score - suf_max) * scale)
    suf_mass = jnp.sum(weights, axis=1, keepdims=True) + new_weight
    suf_acc = jnp.dot(weights.astype(jnp.bfloat16), svbuf[...], preferred_element_type=jnp.float32)
    suf_acc = suf_acc + new_weight.astype(jnp.bfloat16).astype(jnp.float32) * nvbuf[...].astype(
        jnp.float32
    )
    suf_out[:heads] = suf_acc
    suf_out[heads:] = jnp.where(
        lax.broadcasted_iota(jnp.int32, (heads, hd), 1) == 0, suf_max * scale, suf_mass
    )

    pages = tokens // 128
    bias = []
    for half in range(2):
        first = (wide - c + (c + half) % 2) * pages
        for page in range(pages):
            used = jnp.max((ptbuf[...] == first + page).astype(jnp.float32), axis=1, keepdims=True)
            bias.append(jnp.broadcast_to((used - 1.0) * 1e30, (1, 128)))
    bias = jnp.concatenate(bias, axis=1)

    for load in loads[6:]:
        load.wait()
    ktbuf[:, :tokens] = kbuf[0].T
    vbuf[:, :, hd:] = jnp.ones((2, tokens, hd), jnp.bfloat16)

    pl.semaphore_wait(barrier, len(WIDE) + len(TP))

    for a, b in WIDE:
        pltpu.make_async_remote_copy(
            qbuf.at[0, pl.ds(0, heads)],
            qbuf.at[a, pl.ds(b * heads, heads)],
            q_send,
            q_recv.at[a],
            device_id=wide_at(a, b),
            device_id_type=MESH,
        ).start()
    suffix = pltpu.make_async_remote_copy(
        suf_out,
        suf_in,
        suf_send,
        suf_recv,
        device_id=suffix_to,
        device_id_type=MESH,
    )
    pl.when(moved)(suffix.start)

    @pl.when(jnp.logical_not(moved))
    def _():
        suf_in[...] = suf_out[...]

    swaps = [
        pltpu.make_async_remote_copy(
            src,
            dst,
            core_send.at[i],
            core_recv.at[i],
            device_id=partner,
            device_id_type=MESH,
        )
        for i, (src, dst) in enumerate(
            (
                (kbuf.at[0], kbuf.at[1]),
                (vbuf.at[0, :, pl.ds(0, hd)], vbuf.at[1, :, pl.ds(0, hd)]),
                (wbuf.at[0], wbuf.at[1]),
            )
        )
    ]
    for swap in swaps:
        swap.start()
    swaps[0].wait_recv()
    ktbuf[:, tokens:] = kbuf[1].T
    swaps[1].wait_recv()
    values = vbuf[...].reshape(2 * tokens, 2 * hd)

    def landed(ref, sem):
        pltpu.make_async_copy(ref, ref, sem).wait()

    diagonal = lax.broadcasted_iota(jnp.int32, (rows, 128), 0) == lax.broadcasted_iota(
        jnp.int32, (rows, 128), 1
    )

    def line(column):
        return jnp.sum(jnp.where(diagonal, column, 0.0), axis=0, keepdims=True)

    def chunk(a):
        s = jnp.dot(qbuf[a], ktbuf[...], preferred_element_type=jnp.float32) + bias
        top = jnp.max(s, axis=1, keepdims=True)
        p = jnp.exp2((s - top) * scale).astype(jnp.bfloat16)
        acc = jnp.dot(p, values, preferred_element_type=jnp.float32)
        mass = acc[:, hd:]
        acc_out[a] = (acc[:, :hd] / mass).astype(jnp.bfloat16)
        st_out[a] = line(top * scale + jnp.log2(mass))

    def reply(a):
        for b in (4, 3, 5, 2, 6, 1, 7, 0):
            target = join_at(a, b)
            place = pl.ds(b * heads, heads)
            into = pl.ds((a * NZ + b) * heads, heads)

            @pl.when(target[0] != wide)
            def _():
                pltpu.make_async_remote_copy(
                    st_out.at[a],
                    st_in.at[a * NZ + b],
                    st_send,
                    st_recv,
                    device_id=target,
                    device_id_type=MESH,
                ).start()
                pltpu.make_async_remote_copy(
                    acc_out.at[a, place],
                    acc_in.at[into],
                    acc_send,
                    acc_recv,
                    device_id=target,
                    device_id_type=MESH,
                ).start()

            @pl.when(target[0] == wide)
            def _():
                st_in[a * NZ + b] = st_out[a]
                acc_in[into, :] = acc_out[a, place, :]

    for group in GROUPS:
        for a in group:
            landed(qbuf.at[0, pl.ds(heads, rows - heads)] if a == 0 else qbuf.at[a], q_recv.at[a])
        for a in group:
            chunk(a)
        for a in group:
            reply(a)

    spot = lax.broadcasted_iota(jnp.int32, (1, rows), 1) // heads
    joined = []
    landed(st_in.at[pl.ds(0, CHIPS - 1)], st_recv)
    pl.when(moved)(lambda: landed(suf_in, suf_recv))
    suf_acc, suf_max, suf_mass = suf_in[:heads], suf_in[heads:, :1], suf_in[heads:, 1:2]
    for a in range(NY):
        both = st_in[a * NZ]
        for b in range(1, NZ):
            both = jnp.where(spot == b, st_in[a * NZ + b], both)
        joined.append(both)
    best = functools.reduce(jnp.maximum, joined)
    mine = lax.broadcasted_iota(jnp.int32, (heads, rows), 1) % heads == lax.broadcasted_iota(
        jnp.int32, (heads, rows), 0
    )
    row_max = jnp.maximum(
        jnp.max(jnp.where(mine, best, -3e38), axis=1, keepdims=True), suf_max
    )
    spread = [jnp.where(mine, jnp.exp2(both - row_max), 0.0) for both in joined]
    shares = functools.reduce(jnp.add, spread)
    suf_factor = jnp.exp2(suf_max - row_max)
    total = jnp.sum(shares, axis=1, keepdims=True) + suf_mass * suf_factor
    spread = jnp.concatenate(spread, axis=1)
    high = spread.astype(jnp.bfloat16)
    rest = (spread - high.astype(jnp.float32)).astype(jnp.bfloat16)
    factors = jnp.concatenate([high, rest], axis=0)
    landed(acc_in.at[pl.ds(0, (CHIPS - 1) * heads)], acc_recv)
    pre_acc = jnp.dot(factors, acc_in[...], preferred_element_type=jnp.float32)
    summed = pre_acc[:heads] + pre_acc[heads:] + suf_acc * suf_factor
    own_rows = pl.ds(pl.multiple_of((join_y * NZ + join_z) * heads, heads), heads)
    attn_buf[own_rows, :] = (summed / total).astype(jnp.bfloat16)

    def send_rows(device):
        pltpu.make_async_remote_copy(
            attn_buf.at[own_rows],
            attn_buf.at[own_rows],
            attn_send,
            attn_recv.at[join_y],
            device_id=device,
            device_id_type=MESH,
        ).start()

    for plane in (0, 1, 2, 3, 4, 5, 6, 7):
        for a in (2, 1, 3, 0):
            device = ((y + a) % NY * (2 * NZ) + plane * 2 + c, tp)
            if a:
                send_rows(device)
            else:
                pl.when(z != plane)(functools.partial(send_rows, device))
    swaps[2].wait_recv()
    def rows_of(plane):
        sem = attn_recv.at[plane]
        pl.when(join_y == plane)(lambda: landed(attn_buf.at[pl.ds(0, rows - heads)], sem))
        pl.when(join_y != plane)(lambda: landed(attn_buf.at[pl.ds(0, rows)], sem))
        block = slice(plane * rows, (plane + 1) * rows)
        attn32[block, :] = attn_buf[block, :].astype(jnp.float32)

    columns = w_hbm.shape[1]
    share = CHIPS // (NX * NL)

    def project(first, count):
        sums = [jnp.zeros((count, columns), jnp.float32) for _ in range(2)]
        for h in range(0, heads, 2):
            pair = jnp.concatenate(
                [
                    attn32[pl.ds(first * heads + h + i, count, stride=heads), :]
                    for i in range(2)
                ],
                axis=1,
            ).astype(jnp.bfloat16)
            for d in range(2):
                sums[d] = sums[d] + jnp.dot(
                    pair, wbuf[d, h * hd : (h + 2) * hd, :], preferred_element_type=jnp.float32
                )
        for d in range(2):
            for t in range(count // share):
                part = sums[d][t * share : (t + 1) * share]
                proj_out[d, first // share + t] = jnp.concatenate(
                    [part[:, :128], part[:, 128:]], axis=0
                )

    def send_sums(wanted):
        for i, (a, b, d) in enumerate(TP):
            target = tp_at(a, b, d)
            copy = pltpu.make_async_remote_copy(
                proj_out.at[d, target[1]],
                proj_in.at[i],
                proj_send,
                proj_recv,
                device_id=target,
                device_id_type=MESH,
            )
            pl.when(wanted((x + a) % NX))(copy.start)

    for plane in range(2):
        rows_of(plane)
        project(plane * NZ, NZ)
        send_sums(lambda to: to == plane)
    for plane in range(2, NY):
        rows_of(plane)
    project(2 * NZ, CHIPS - 2 * NZ)
    send_sums(lambda to: to > 1)
    landed(proj_in, proj_recv)
    parts = [proj_out[0, tp], jnp.zeros((8, 128), jnp.float32)]
    for i, (a, b, d) in enumerate(TP):
        parts[d] = parts[d] + proj_in[i]
    for core in range(2):
        half = jnp.where(c == core, parts[0], parts[1])
        for i in range(share):
            for j in range(2):
                o_ref[2 * i + core : 2 * i + core + 1, j * 128 : (j + 1) * 128] = half[
                    j * share + i : j * share + i + 1
                ]

    landed(qbuf.at[pl.ds(0, NY - 1)], q_send)
    landed(qbuf.at[0, pl.ds(heads, rows - heads)], q_send)
    for swap in swaps:
        swap.wait_send()
    landed(acc_out.at[pl.ds(0, NY - 1)], acc_send)
    landed(acc_out.at[0, pl.ds(heads, rows - heads)], acc_send)
    landed(st_in.at[pl.ds(0, CHIPS - 1)], st_send)
    pl.when(moved)(suffix.wait_send)
    landed(attn_buf.at[pl.ds(0, (CHIPS - 1) * heads)], attn_send)
    landed(proj_in, proj_send)


def local(
    queries,
    new_keys,
    new_values,
    prefix_keys,
    prefix_values,
    suffix_keys,
    suffix_values,
    lengths,
    page_table,
    out_weight,
):
    _, heads, hd = queries.shape
    tokens = prefix_keys.shape[0] * prefix_keys.shape[1]
    slots = suffix_keys.shape[1]
    depth, columns = out_weight.shape
    rows = NZ * heads
    bf16, f32 = jnp.bfloat16, jnp.float32
    dma = pltpu.SemaphoreType.DMA
    return pl.pallas_call(
        kernel,
        out_shape=pltpu.VMEM((8, columns), f32),
        in_specs=[pl.BlockSpec(memory_space=pltpu.SMEM)] + [pl.BlockSpec(memory_space=pl.ANY)] * 9,
        out_specs=pl.BlockSpec(memory_space=pltpu.VMEM),
        scratch_shapes=[
            pltpu.VMEM((NY, rows, hd), bf16),
            pltpu.VMEM((2, tokens, hd), bf16),
            pltpu.VMEM((2, tokens, 2 * hd), bf16),
            pltpu.VMEM((hd, 2 * tokens), bf16),
            pltpu.VMEM((slots, hd), bf16),
            pltpu.VMEM((slots, hd), bf16),
            pltpu.VMEM((1, hd), bf16),
            pltpu.VMEM((1, hd), bf16),
            pltpu.VMEM((1, page_table.shape[0]), jnp.int32),
            pltpu.VMEM((2, depth, columns), bf16),
            pltpu.VMEM((NY, rows, hd), bf16),
            pltpu.VMEM((NY, 1, rows), f32),
            pltpu.VMEM((CHIPS * heads, hd), bf16),
            pltpu.VMEM((CHIPS, 1, rows), f32),
            pltpu.VMEM((2 * heads, hd), f32),
            pltpu.VMEM((2 * heads, hd), f32),
            pltpu.VMEM((CHIPS * heads, hd), bf16),
            pltpu.VMEM((CHIPS * heads, hd), f32),
            pltpu.VMEM((2, NX * NL, 8, 128), f32),
            pltpu.VMEM((len(TP), 8, 128), f32),
            dma((9,)),
            dma,
            dma((NY,)),
            dma((3,)),
            dma((3,)),
            dma,
            dma,
            dma,
            dma,
            dma,
            dma,
            dma,
            dma((NY,)),
            dma,
            dma,
        ],
        compiler_params=pltpu.CompilerParams(
            collective_id=0, has_side_effects=True, vmem_limit_bytes=32 * 1024 * 1024
        ),
        name="attention_step",
    )(
        lengths,
        *(
            pltpu.with_memory_space_constraint(a, pltpu.HBM)
            for a in (
                queries.reshape(heads, hd),
                new_keys.reshape(1, hd),
                new_values.reshape(1, hd),
                prefix_keys.reshape(tokens, hd),
                prefix_values.reshape(tokens, hd),
                suffix_keys.reshape(slots, hd),
                suffix_values.reshape(slots, hd),
                page_table.reshape(1, -1),
                out_weight,
            )
        ),
    )


def solution(mesh):
    in_specs = (
        P("wide", "tp", None),
        P("wide", "tp", None),
        P("wide", "tp", None),
        P("wide", None, "tp", None),
        P("wide", None, "tp", None),
        P("wide", None, "tp", None),
        P("wide", None, "tp", None),
        P("wide"),
        P(),
        P("tp", "wide"),
    )
    out_specs = P("tp", "wide")
    return jax.shard_map(local, mesh=mesh, in_specs=in_specs, out_specs=out_specs, check_vma=False)
```
